256 devices in a mesh: segment: 8 (over y, x_hi), dp: 32 (over z, x_lo, core).
Axes of the slice: x: 4 (x_hi: 2, x_lo: 2; x = x_hi * 2 + x_lo), y: 4, z: 8, core: 2. Of those that a mesh axis runs over, the one named last changes fastest.
Arguments:
- features: bfloat16 [128, 144, 512], P('dp'), may hold values from -6 to 6
- labels: int32 [128], P('dp'), may hold values from 0 to 3
- classifier: float32 [512, 4], replicated, may hold values from -1.5 to 1.5
- w_mix: bfloat16 [24, 512, 512], P('segment'), may hold values from -0.25 to 0.25
- w_point: bfloat16 [24, 512, 512], P('segment'), may hold values from -0.25 to 0.25
- kernels: bfloat16 [24, 9, 512], P('segment'), may hold values from -2 to 2
- counts: int32 [8], P('segment'), may hold values from 1 to 3, 20 in all
Outputs:
- grad_mix: float32 [24, 512, 512], P('segment')
- grad_point: float32 [24, 512, 512], P('segment')
- grad_kernel: float32 [24, 9, 512], P('segment')
The draws below stay inside these ranges and needn't reach their ends.
Inputs may be any that keep to these rules, and one draw needn't show every extreme that they name: Section s holds counts[s] cells; together 20, the largest 3.
All inputs are finite; a program needn't handle non-finite values. No bound on the sum of `counts` on one device may be relied on, other than what follows from the above.
Results may differ from the reference program's by a relative error of at most 0.012.
Values may be sent and summed in bfloat16 or wider, within the bound.
A program may use at most 128 MiB of HBM per device.

```python
import math
import jax
import jax.numpy as jnp
import numpy as np
from jax import lax

CH = 512
CLASSES = 4
GRID = 12
SLOTS = 3
PIX = 144
BATCH = 128
CELL_SLOTS = 24
TOTAL_CELLS = 20
N_SEGMENT = 8


def place_ends(entries, rng, low, top_value):
    extent = entries.shape
    spot = [jax.random.randint(jax.random.fold_in(rng, axis), (), 0, extent[axis]) for axis in range(len(extent))]
    entries = entries.at[tuple(spot)].set(low)
    longest = extent.index(max(extent))
    spot[longest] = (spot[longest] + 1) % extent[longest]
    return entries.at[tuple(spot)].set(top_value)


def strengthened(values, stream_key, source, target, blocks, factor):
    def block_of(dim):
        return (jnp.arange(values.shape[dim]) // (values.shape[dim] // blocks)).reshape((-1,) + (1,) * (values.ndim - 1 - dim))

    one_side = jax.random.permutation(stream_key, blocks)[block_of(target)]
    other_side = (block_of(target) + blocks // 2) % blocks
    return jnp.where((block_of(source) == one_side) | (block_of(source) == other_side), factor * values, values)


def level_of(stream_key, dims, pieces, low, top_value):
    factor_of, own = 1.0, jax.random.fold_in(stream_key, 6)
    for dim, shards_of in pieces:
        draws = jnp.exp(jax.random.uniform(jax.random.fold_in(own, dim), (shards_of,), jnp.float32, low / len(pieces), top_value / len(pieces)))
        factor_of = factor_of * jnp.repeat(draws, dims[dim] // shards_of).reshape([-1 if axis == dim else 1 for axis in range(len(dims))])
    return factor_of


def split_up(number_of, total, limit, skew):
    loads = [(1 << 20) // math.isqrt(standing ** skew) + 1 for standing in range(2, number_of + 1)]
    spare, given = total - limit - (number_of - 1), [1] * (number_of - 1)
    while spare > 0:
        candidates = [i for i in range(number_of - 1) if given[i] < limit]
        whole, remaining = sum([loads[i] for i in candidates]), spare
        for i in candidates:
            addition = min(limit - given[i], max(1, remaining * loads[i] // whole), spare)
            given[i] = given[i] + addition
            spare = spare - addition
    return np.array([limit] + given)


def ragged_sizes(stream_key, count, total, reach, lean):
    if count == 2:
        one = jax.random.randint(stream_key, (), max(1, total - reach), min(reach, total - 1) + 1)
        return jnp.stack([one, total - one])
    tallies = jnp.asarray(split_up(count, total, reach, lean), jnp.int32)
    pairs = (count - 1) // 2
    donor, sink = tallies[1:1 + 2 * pairs:2], tallies[2:2 + 2 * pairs:2]
    room = jnp.minimum(donor - 1, reach - sink)
    shifted = jax.random.randint(jax.random.fold_in(stream_key, 1), (pairs,), 0, 1 << 20) % (room + 1)
    tallies = tallies.at[1:1 + 2 * pairs:2].set(donor - shifted).at[2:2 + 2 * pairs:2].set(sink + shifted)
    return tallies[jax.random.permutation(jax.random.fold_in(stream_key, 2), count)]


def centred(stream_key, shape, deviation, limit, pieces=(), kind=jnp.bfloat16):
    factor_of = level_of(stream_key, shape, pieces, -0.22, 0.18) if pieces else 1.0
    entries = jax.random.normal(stream_key, shape, jnp.float32) * deviation * factor_of
    return jnp.minimum(jnp.maximum(entries, -limit), limit).astype(kind)


def noise_with(key, extent, deviation, bound, split, heavy, kind=jnp.bfloat16):
    result = deviation * jax.random.normal(key, extent, jnp.float32)
    if split:
        result = result * level_of(key, extent, split, -0.22, 0.18)
    return jnp.clip(strengthened(result, jax.random.fold_in(key, 3), *heavy), -bound, bound).astype(kind)


def setup_inputs(seed: int = 0) -> dict:
    seeds = jax.random.split(jax.random.key(seed), 8)
    return {
        "features": noise_with(seeds[0], (BATCH, PIX, CH), 1.0, 6.0, ((0, 32),), (0, 2, 32, 2.75)),
        "labels": place_ends(jax.random.randint(seeds[1], (BATCH,), 0, CLASSES), jax.random.fold_in(seeds[1], 1), 0, CLASSES - 1).astype(jnp.int32),
        "classifier": centred(seeds[2], (CH, CLASSES), 0.25, 1.5, (), jnp.float32),
        "w_mix": centred(seeds[3], (CELL_SLOTS, CH, CH), CH ** -0.5, 0.25, ((0, 8),)),
        "w_point": centred(seeds[4], (CELL_SLOTS, CH, CH), CH ** -0.5, 0.25, ((0, 8),)),
        "kernels": centred(seeds[5], (CELL_SLOTS, 9, CH), 9 ** -0.5, 2.0, ((0, 8),)),
        "counts": ragged_sizes(seeds[6], N_SEGMENT, TOTAL_CELLS, SLOTS, 1).astype(jnp.int32),
    }


EPSILON = 1e-06

def flatten_rows(values):
    return values.reshape(-1, values.shape[-1])

def depthwise(rectified, kernel_row, grid_side):
    shape_in = rectified.shape
    image = rectified.astype(jnp.float32).reshape(shape_in[:-2] + (grid_side, grid_side, shape_in[-1]))
    padded = jnp.pad(image, [(0, 0)] * (image.ndim - 3) + [(1, 1), (1, 1), (0, 0)])
    taps = kernel_row.astype(jnp.float32)
    total = jnp.zeros(image.shape, jnp.float32)
    for row_off in range(3):
        for col_off in range(3):
            total = total + taps[3 * row_off + col_off] * padded[..., row_off:row_off + grid_side, col_off:col_off + grid_side, :]
    return total.reshape(shape_in)

def depthwise_back(rectified, kernel_row, upstream, grid_side):
    shape_in = rectified.shape
    image = rectified.astype(jnp.float32).reshape(shape_in[:-2] + (grid_side, grid_side, shape_in[-1]))
    padding = [(0, 0)] * (image.ndim - 3) + [(1, 1), (1, 1), (0, 0)]
    padded_in = jnp.pad(image, padding)
    upstream_img = upstream.reshape(image.shape)
    padded_up = jnp.pad(upstream_img, padding)
    taps = kernel_row.astype(jnp.float32)
    summed_axes = tuple(range(image.ndim - 1))
    tap_grads = []
    input_grad = jnp.zeros(image.shape, jnp.float32)
    for row_off in range(3):
        for col_off in range(3):
            window = padded_in[..., row_off:row_off + grid_side, col_off:col_off + grid_side, :]
            tap_grads.append(lax.optimization_barrier(jnp.sum(window * upstream_img, axis=summed_axes)))
            moved = padded_up[..., 2 - row_off:2 - row_off + grid_side, 2 - col_off:2 - col_off + grid_side, :]
            input_grad = input_grad + taps[3 * row_off + col_off] * moved
    return (jnp.stack(tap_grads), input_grad.reshape(shape_in))

def cell_forward(prev_act, older_act, mix_weight, point_weight, kernel_row, grid_side):
    rect_prev = jax.nn.relu(prev_act)
    rect_older = jax.nn.relu(older_act)
    separable = depthwise(rect_older, kernel_row, grid_side).astype(jnp.bfloat16)
    branches = jnp.dot(flatten_rows(separable), point_weight, preferred_element_type=jnp.float32)
    branches = branches + jnp.dot(flatten_rows(rect_prev), mix_weight, preferred_element_type=jnp.float32)
    summed = prev_act.astype(jnp.float32) + branches.reshape(prev_act.shape)
    scale = lax.rsqrt(lax.optimization_barrier(jnp.mean(summed * summed, axis=-1, keepdims=True)) + EPSILON)
    return ((summed * scale).astype(jnp.bfloat16), separable, summed)

def cell_backward(prev_act, older_act, separable, summed, mix_weight, point_weight, kernel_row, grad_new, grad_pass, grid_side):
    scale = lax.rsqrt(lax.optimization_barrier(jnp.mean(summed * summed, axis=-1, keepdims=True)) + EPSILON)
    normed = summed * scale
    grad_norm = grad_new.astype(jnp.float32)
    grad_sum = scale * (grad_norm - normed * lax.optimization_barrier(jnp.mean(grad_norm * normed, axis=-1, keepdims=True)))
    grad_half = grad_sum.astype(jnp.bfloat16)
    rows_grad = flatten_rows(grad_half)
    point_grad = jnp.dot(flatten_rows(separable).T, rows_grad, preferred_element_type=jnp.float32)
    mix_grad = jnp.dot(flatten_rows(jax.nn.relu(prev_act)).T, rows_grad, preferred_element_type=jnp.float32)
    sep_grad = jnp.dot(rows_grad, point_weight.T, preferred_element_type=jnp.float32).reshape(prev_act.shape)
    prev_mix = jnp.dot(rows_grad, mix_weight.T, preferred_element_type=jnp.float32).reshape(prev_act.shape)
    grad_prev = (grad_sum + jnp.where(prev_act > 0, prev_mix, 0.0) + grad_pass.astype(jnp.float32)).astype(jnp.bfloat16)
    kernel_grad, older_rect = depthwise_back(jax.nn.relu(older_act), kernel_row, sep_grad, grid_side)
    grad_older = jnp.where(older_act > 0, older_rect, 0.0).astype(jnp.bfloat16)
    return (grad_prev, grad_older, mix_grad, point_grad, kernel_grad)

def head_grad(final_act, image_labels, classifier):
    pooled = lax.optimization_barrier(jnp.mean(jax.nn.relu(final_act).astype(jnp.float32), axis=-2))
    logits = jnp.dot(pooled, classifier, precision=lax.Precision.HIGHEST)
    classes = jnp.arange(classifier.shape[1], dtype=jnp.int32)
    onehot = (image_labels[..., None] == classes).astype(jnp.float32)
    grad_pool = jnp.dot(logits - onehot, classifier.T, precision=lax.Precision.HIGHEST)
    return jnp.where(final_act > 0, grad_pool[..., None, :] / final_act.shape[-2], 0.0).astype(jnp.bfloat16)

def reference(features, labels, classifier, w_mix, w_point, kernels, counts):
    prev_act = features
    older_act = features
    saved = []
    for segment in range(N_SEGMENT):
        for slot in range(SLOTS):
            index = segment * SLOTS + slot
            active = slot < counts[segment]
            new_act, separable, summed = cell_forward(prev_act, older_act, w_mix[index], w_point[index], kernels[index], GRID)
            saved.append((prev_act, older_act, separable, summed))
            prev_act, older_act = (jnp.where(active, new_act, prev_act), jnp.where(active, prev_act, older_act))
    grad_prev = head_grad(prev_act, labels, classifier)
    grad_older = jnp.zeros_like(grad_prev)
    mix_list = [None] * (N_SEGMENT * SLOTS)
    point_list = [None] * (N_SEGMENT * SLOTS)
    kernel_list = [None] * (N_SEGMENT * SLOTS)
    for index in reversed(range(N_SEGMENT * SLOTS)):
        active = index % SLOTS < counts[index // SLOTS]
        prev_in, older_in, separable, summed = saved[index]
        new_prev, new_older, mix_grad, point_grad, kernel_grad = cell_backward(prev_in, older_in, separable, summed, w_mix[index], w_point[index], kernels[index], grad_prev, grad_older, GRID)
        grad_prev = jnp.where(active, new_prev, grad_prev)
        grad_older = jnp.where(active, new_older, grad_older)
        mix_list[index] = jnp.where(active, mix_grad, 0.0)
        point_list[index] = jnp.where(active, point_grad, 0.0)
        kernel_list[index] = jnp.where(active, kernel_grad, 0.0)
    return (jnp.stack(mix_list), jnp.stack(point_list), jnp.stack(kernel_list))
```

```python
import functools

import jax
import jax.numpy as jnp
from jax import lax
from jax.experimental import pallas as pl
from jax.experimental.pallas import tpu as pltpu
from jax.sharding import PartitionSpec as P

GRID = 12
PITCH = 16
ROWS = GRID * PITCH
CH = 512
CELLS = 12
EPSILON = 1e-06
MESH = pl.DeviceIdType.MESH
BF = jnp.bfloat16
F32 = jnp.float32


def place():
    seg, dp = lax.axis_index("segment"), lax.axis_index("dp")
    y, xh = seg // 2, seg % 2
    core, xl, z = dp % 2, (dp // 2) % 2, dp // 4
    return seg, dp, y, xh, z, xl, core


def dev(y, xh, z, xl, core):
    return (y * 2 + xh, (z * 2 + xl) * 2 + core)


def neighbours():
    seg, dp, y, xh, z, xl, core = place()
    yp = y + 1 - 2 * (y % 2)
    return {
        "core": dev(y, xh, z, xl, 1 - core),
        "xs": dev(y, xh, z, 1 - xl, core),
        "xd": dev(y, 1 - xh, z, 1 - xl, core),
        "x+": dev(y, jnp.where(xl == 0, xh, 1 - xh), z, 1 - xl, core),
        "x-": dev(y, jnp.where(xl == 1, xh, 1 - xh), z, 1 - xl, core),
        "z+": dev(y, xh, (z + 1) % 8, xl, core),
        "z-": dev(y, xh, (z + 7) % 8, xl, core),
        "y": dev(yp, xh, z, xl, core),
        "hop": dev(3 - y, xh, z, xl, core),
    }


def greet(names, near):
    barrier = pltpu.get_barrier_semaphore()
    for name in names:
        pl.semaphore_signal(barrier, inc=1, device_id=near[name], device_id_type=MESH)
    pl.semaphore_wait(barrier, len(names))


def remote(src, dst, send, recv, i, target):
    return pltpu.make_async_remote_copy(
        src_ref=src, dst_ref=dst, send_sem=send.at[i], recv_sem=recv.at[i], device_id=target, device_id_type=MESH
    )


def gather_kernel(mix_ref, point_ref, small_ref, w_ref, s_ref, send, recv, local):
    _, _, y, xh, z, xl, core = place()
    near = neighbours()
    yl, zp = y % 2, z % 2
    own = yl * 2 + xh
    sec_y, sec_x, sec_xy = (1 - yl) * 2 + xh, yl * 2 + (1 - xh), (1 - yl) * 2 + (1 - xh)
    loc = [
        pltpu.make_async_copy(mix_ref, w_ref.at[0, pl.ds(own * 3, 3)], local.at[0]),
        pltpu.make_async_copy(point_ref, w_ref.at[1, pl.ds(own * 3, 3)], local.at[1]),
        pltpu.make_async_copy(small_ref, s_ref.at[pl.ds(own * 3, 3)], local.at[2]),
    ]
    for c in loc:
        c.start()
    greet(("core", "xs", "xd", "z+", "z-", "y"), near)
    for c in loc:
        c.wait()

    def piece(i, sec, row, count, name):
        at = w_ref.at[core, pl.ds(sec * 3, 3), pl.ds(pl.multiple_of(row, 16), count)]
        return remote(at, at, send, recv, i, near[name])

    def tiny(i, sec, name):
        at = s_ref.at[pl.ds(sec * 3, 3)]
        return remote(at, at, send, recv, i, near[name])

    mine, other = 128 * (2 * zp + xl), 128 * (2 * zp + 1 - xl)
    t = {
        0: piece(0, own, 256 * zp, 256, "y"),
        1: piece(1, own, other, 128, "xd"),
        2: piece(2, sec_x, mine, 128, "xs"),
        3: piece(3, sec_x, mine, 64, "z+"),
        4: piece(4, sec_x, mine + 64, 64, "z-"),
        5: piece(5, sec_y, other, 128, "xd"),
        6: piece(6, sec_y, 256 * zp, 128, "z+"),
        7: piece(7, sec_y, 256 * zp + 128, 128, "z-"),
        8: piece(8, sec_xy, mine, 128, "xs"),
        9: piece(9, sec_xy, mine, 64, "z+"),
        10: piece(10, sec_xy, mine + 64, 64, "z-"),
        11: piece(11, sec_x, other, 64, "z+"),
        12: piece(12, sec_x, other + 64, 64, "z-"),
        13: piece(13, sec_xy, other, 64, "z+"),
        14: piece(14, sec_xy, other + 64, 64, "z-"),
        15: piece(15, sec_y, 256 * zp, 256, "core"),
        16: piece(16, sec_y, 256 * (1 - zp), 256, "core"),
        17: piece(17, sec_x, 256 * zp, 256, "core"),
        18: piece(18, sec_x, 256 * (1 - zp), 256, "core"),
        19: piece(19, sec_xy, 256 * zp, 256, "core"),
        20: piece(20, sec_xy, 256 * (1 - zp), 256, "core"),
        21: tiny(21, own, "y"),
        22: tiny(22, own, "xd"),
        23: tiny(23, sec_y, "xd"),
    }

    def go(*ids):
        for i in ids:
            t[i].start()

    def got(*ids):
        for i in ids:
            t[i].wait_recv()

    go(21, 22, 1, 0)
    got(21)
    go(23)
    got(1)
    go(2, 3, 4)
    got(0)
    go(5, 6, 7, 15)
    got(2)
    go(11, 12, 17)
    got(5)
    go(8, 9, 10)
    got(6, 7)
    go(16)
    got(8)
    go(13, 14, 19)
    got(3, 4, 11, 12)
    go(18)
    got(9, 10, 13, 14)
    go(20)
    got(22, 23, 15, 16, 17, 18, 19, 20)
    for i in range(24):
        t[i].wait_send()


def gather(w_mix, w_point, small):
    return pl.pallas_call(
        gather_kernel,
        out_shape=(
            jax.ShapeDtypeStruct((2, CELLS, CH, CH), BF),
            jax.ShapeDtypeStruct((CELLS, 16, CH), BF),
        ),
        in_specs=[pl.BlockSpec(memory_space=pl.ANY)] * 3,
        out_specs=(pl.BlockSpec(memory_space=pl.ANY),) * 2,
        scratch_shapes=[
            pltpu.SemaphoreType.DMA((24,)),
            pltpu.SemaphoreType.DMA((24,)),
            pltpu.SemaphoreType.DMA((3,)),
        ],
        compiler_params=pltpu.CompilerParams(collective_id=1, has_side_effects=True),
        name="gather",
    )(w_mix, w_point, small)


def hop_kernel(x_ref, o_ref, send, recv):
    near = neighbours()
    greet(("hop",), near)
    copies = [remote(x_ref.at[i], o_ref.at[i], send, recv, i, near["hop"]) for i in range(2)]
    for c in copies:
        c.start()
    for c in copies:
        c.wait()


def hop(x):
    return pl.pallas_call(
        hop_kernel,
        out_shape=jax.ShapeDtypeStruct(x.shape, x.dtype),
        in_specs=[pl.BlockSpec(memory_space=pl.ANY)],
        out_specs=pl.BlockSpec(memory_space=pl.ANY),
        scratch_shapes=[pltpu.SemaphoreType.DMA((2,)), pltpu.SemaphoreType.DMA((2,))],
        compiler_params=pltpu.CompilerParams(collective_id=2, has_side_effects=True),
        name="hop",
    )(x)


def down(r):
    return jnp.concatenate([jnp.zeros((PITCH, r.shape[1]), r.dtype), r[:-PITCH]], axis=0)


def up(r):
    return jnp.concatenate([r[PITCH:], jnp.zeros((PITCH, r.shape[1]), r.dtype)], axis=0)


def fwd_kernel(save, flags, xa_ref, xb_ref, w_ref, k_ref, *rest):
    if save:
        c_ref, o_ref, sp_ref, so_ref, ss_ref, st_ref, hg_ref, sep = rest
    else:
        o_ref, sep = rest
    i = pl.program_id(0)

    @pl.when(i == 0)
    def _():
        @pl.when(flags[CELLS] == 0)
        def _():
            o_ref[0] = xa_ref[...]
            o_ref[1] = xa_ref[...]

        @pl.when(flags[CELLS] != 0)
        def _():
            o_ref[...] = xb_ref[...]

    @pl.when(flags[i] == 1)
    def _():
        if save:
            sp_ref[0] = o_ref[0]
            so_ref[0] = o_ref[1]
        real = lax.broadcasted_iota(jnp.int32, (ROWS, 128), 0) % PITCH < GRID
        for c in range(4):
            cols = slice(128 * c, 128 * c + 128)
            a = jnp.maximum(o_ref[1, :, cols].astype(F32), 0.0)
            k = k_ref[0, :, cols].astype(F32)
            am, ap = pltpu.roll(a, 1, 0), pltpu.roll(a, ROWS - 1, 0)
            r = [k[3 * u : 3 * u + 1] * am + k[3 * u + 1 : 3 * u + 2] * a + k[3 * u + 2 : 3 * u + 3] * ap for u in range(3)]
            s = r[1] + down(r[0]) + up(r[2])
            sep[:, cols] = jnp.where(real, s, 0.0).astype(BF)
        if save:
            ss_ref[0] = sep[...]
        prev = o_ref[0]
        total = jnp.dot(sep[...], w_ref[1, 0], preferred_element_type=F32)
        total = total + jnp.dot(jnp.maximum(prev, 0), w_ref[0, 0], preferred_element_type=F32)
        total = prev.astype(F32) + total
        q = lax.rsqrt(jnp.mean(total * total, axis=-1, keepdims=True) + EPSILON)
        if save:
            st_ref[0] = total
        o_ref[1] = prev
        o_ref[0] = (total * q).astype(BF)

    if save:

        @pl.when(i == CELLS - 1)
        def _():
            last = o_ref[0]
            pooled = jnp.sum(jnp.maximum(last.astype(F32), 0.0), axis=0, keepdims=True) / (GRID * GRID)
            grad = jnp.zeros((1, CH), F32)
            for k in range(4):
                row = c_ref[k : k + 1, :]
                logit = jnp.sum(pooled * row, axis=-1, keepdims=True)
                hot = jnp.where(flags[CELLS + 1] == k, 1.0, 0.0)
                grad = grad + (logit - hot) * row
            grad = grad / (GRID * GRID)
            hg_ref[0] = jnp.where(last > 0, jnp.broadcast_to(grad, last.shape), 0.0).astype(BF)
            hg_ref[1] = jnp.zeros((ROWS, CH), BF)


def forward(flags, image, arrived, weights, small, classes, save):
    whole = lambda n: pl.BlockSpec(n, lambda i, f: (0,) * len(n))
    one = lambda n: pl.BlockSpec((1,) + n, lambda i, f: (i, 0, 0))
    pair = jax.ShapeDtypeStruct((2, ROWS, CH), BF)
    in_specs = [
        whole((ROWS, CH)),
        whole((2, ROWS, CH)),
        pl.BlockSpec((2, 1, CH, CH), lambda i, f: (0, i, 0, 0)),
        one((16, CH)),
    ]
    out_specs, out_shape = [whole((2, ROWS, CH))], [pair]
    args = [flags, image, arrived, weights, small]
    if save:
        in_specs.append(whole((8, CH)))
        args.append(classes)
        out_specs += [one((ROWS, CH))] * 4 + [whole((2, ROWS, CH))]
        kept = jax.ShapeDtypeStruct((CELLS, ROWS, CH), BF)
        out_shape += [kept, kept, kept, jax.ShapeDtypeStruct((CELLS, ROWS, CH), F32), pair]
    return pl.pallas_call(
        functools.partial(fwd_kernel, save),
        grid_spec=pltpu.PrefetchScalarGridSpec(
            num_scalar_prefetch=1,
            grid=(CELLS,),
            in_specs=in_specs,
            out_specs=out_specs,
            scratch_shapes=[pltpu.VMEM((ROWS, CH), BF)],
        ),
        out_shape=out_shape,
        compiler_params=pltpu.CompilerParams(vmem_limit_bytes=32 << 20),
        name="forward_save" if save else "forward",
    )(*args)


NT = (((1,), (1,)), ((), ()))
TN = (((0,), (0,)), ((), ()))


def bwd_kernel(wgrad, flags, ga_ref, gb_ref, w_ref, k_ref, sp_ref, so_ref, ss_ref, st_ref, *rest):
    if wgrad:
        gw_ref, gk_ref, o_ref, gs = rest
    else:
        o_ref, gs = rest
    i = pl.program_id(0)
    cell = CELLS - 1 - i

    @pl.when(i == 0)
    def _():
        @pl.when(flags[CELLS] == 0)
        def _():
            o_ref[...] = ga_ref[...]

        @pl.when(flags[CELLS] != 0)
        def _():
            o_ref[...] = gb_ref[...]

    @pl.when(flags[cell] == 1)
    def _():
        total = st_ref[0]
        q = lax.rsqrt(jnp.mean(total * total, axis=-1, keepdims=True) + EPSILON)
        n = total * q
        gn = o_ref[0].astype(F32)
        gt = q * (gn - n * jnp.mean(gn * n, axis=-1, keepdims=True))
        gh = gt.astype(BF)
        gs[...] = lax.dot_general(gh, w_ref[1, 0], NT, preferred_element_type=F32)
        gm = lax.dot_general(gh, w_ref[0, 0], NT, preferred_element_type=F32)
        prev = sp_ref[0]
        o_ref[0] = (gt + jnp.where(prev > 0, gm, 0.0) + o_ref[1].astype(F32)).astype(BF)
        for c in range(4):
            cols = slice(128 * c, 128 * c + 128)
            g = gs[:, cols]
            k = k_ref[0, :, cols].astype(F32)
            gv = [pltpu.roll(g, ROWS - 1, 0), g, pltpu.roll(g, 1, 0)]
            r = [
                k[3 * u : 3 * u + 1] * gv[0] + k[3 * u + 1 : 3 * u + 2] * gv[1] + k[3 * u + 2 : 3 * u + 3] * gv[2]
                for u in range(3)
            ]
            rel = r[1] + up(r[0]) + down(r[2])
            older = so_ref[0, :, cols]
            o_ref[1, :, cols] = jnp.where(older > 0, rel, 0.0).astype(BF)
            if wgrad:
                a = jnp.maximum(older.astype(F32), 0.0)
                for v in range(3):
                    gk_ref[0, v : v + 1, cols] = jnp.sum(a[:-PITCH] * gv[v][PITCH:], axis=0, keepdims=True)
                    gk_ref[0, 3 + v : 4 + v, cols] = jnp.sum(a * gv[v], axis=0, keepdims=True)
                    gk_ref[0, 6 + v : 7 + v, cols] = jnp.sum(a[PITCH:] * gv[v][:-PITCH], axis=0, keepdims=True)
        if wgrad:
            gw_ref[0, 0] = lax.dot_general(jnp.maximum(prev, 0), gh, TN, preferred_element_type=F32).astype(BF)
            gw_ref[1, 0] = lax.dot_general(ss_ref[0], gh, TN, preferred_element_type=F32).astype(BF)

    if wgrad:

        @pl.when(flags[cell] != 1)
        def _():
            gw_ref[...] = jnp.zeros_like(gw_ref)
            gk_ref[...] = jnp.zeros_like(gk_ref)


def backward(flags, arrived, head, weights, small, saved, wgrad):
    whole = lambda n: pl.BlockSpec(n, lambda i, f: (0,) * len(n))
    one = lambda n: pl.BlockSpec((1,) + n, lambda i, f: (CELLS - 1 - i, 0, 0))
    both = pl.BlockSpec((2, 1, CH, CH), lambda i, f: (0, CELLS - 1 - i, 0, 0))
    out_specs, out_shape = [whole((2, ROWS, CH))], [jax.ShapeDtypeStruct((2, ROWS, CH), BF)]
    if wgrad:
        out_specs = [both, one((16, CH))] + out_specs
        out_shape = [
            jax.ShapeDtypeStruct((2, CELLS, CH, CH), BF),
            jax.ShapeDtypeStruct((CELLS, 16, CH), F32),
        ] + out_shape
    return pl.pallas_call(
        functools.partial(bwd_kernel, wgrad),
        grid_spec=pltpu.PrefetchScalarGridSpec(
            num_scalar_prefetch=1,
            grid=(CELLS,),
            in_specs=[whole((2, ROWS, CH)), whole((2, ROWS, CH)), both, one((16, CH))] + [one((ROWS, CH))] * 4,
            out_specs=out_specs,
            scratch_shapes=[pltpu.VMEM((ROWS, CH), F32)],
        ),
        out_shape=out_shape,
        compiler_params=pltpu.CompilerParams(vmem_limit_bytes=32 << 20),
        name="backward_weights" if wgrad else "backward",
    )(flags, arrived, head, weights, small, *saved)


def sum_kernel(g_ref, o_ref, acc, rb, zp0, zp, xp0, xp, ap0, ap, bp0, bp, yb, ob, send, recv, local):
    _, _, y, xh, z, xl, core = place()
    near = neighbours()
    yl = y % 2
    count = [0]
    sends = []

    def move(src, dst, name):
        c = remote(src, dst, send, recv, count[0], near[name])
        count[0] += 1
        sends.append(c)
        c.start()
        return c

    load = pltpu.make_async_copy(g_ref.at[core], acc, local.at[0])
    load.start()
    greet(("core", "xs", "xd", "z+", "z-", "y"), near)
    twin = [move(g_ref.at[1 - core, a, b], rb.at[a, b], "core") for a in range(2) for b in range(2)]
    load.wait()
    for j in range(4):
        a, b = j // 2, j % 2
        twin[j].wait_recv()

        def add(n, _, a=a, b=b):
            s, zz = n // 8, n % 8
            acc[a, b, s, zz] = (acc[a, b, s, zz].astype(F32) + rb[a, b, s, zz].astype(F32)).astype(BF)
            return 0

        lax.fori_loop(0, 24, add, 0)

    def plus(ref, *others):
        def step(s, _):
            v = ref[:, s].astype(F32)
            for o in others:
                v = v + o[:, s].astype(F32)
            ref[:, s] = v.astype(BF)
            return 0

        lax.fori_loop(0, 3, step, 0)

    def zat(d):
        return (z + 8 + d) % 8

    def xat(d):
        x = (xh * 2 + xl + 4 + d) % 4
        return x // 2, x % 2

    def a1(d):
        return acc.at[:, :, :, zat(d), 0]

    def b1(d):
        h, l = xat(d)
        return acc.at[:, h, :, :, 1, l]

    def a2(d):
        h, l = xat(d)
        return acc.at[:, h, :, z, 0, l]

    def b2(d):
        return acc.at[:, xh, :, zat(d), 1, xl]

    def plus4(ref, *others):
        def step(n, _):
            a, b = n // 2, n % 2
            v = ref[a, b].astype(F32)
            for o in others:
                v = v + o[a, b].astype(F32)
            ref[a, b] = v.astype(BF)
            return 0

        lax.fori_loop(0, 4, step, 0)

    za = [move(a1(4).at[:, :, :, 0], zp0.at[0], "z+"), move(a1(4).at[:, :, :, 1], zp0.at[1], "z-")]
    xa = [move(b1(2).at[0], xp0.at[0], "x+"), move(b1(2).at[1], xp0.at[1], "x-")]

    for c in za:
        c.wait_recv()
    plus4(a1(3).at[:, :, :, 0], zp0.at[0])
    plus4(a1(-3).at[:, :, :, 1], zp0.at[1])
    za = [move(a1(3), zp.at[0, 0], "z+"), move(a1(-3), zp.at[0, 1], "z-")]

    for c in xa:
        c.wait_recv()

    def plus1(ref, other):
        def step(s, _):
            ref[s] = (ref[s].astype(F32) + other[s].astype(F32)).astype(BF)
            return 0

        lax.fori_loop(0, 3, step, 0)

    plus1(b1(1).at[0], xp0.at[0])
    plus1(b1(-1).at[1], xp0.at[1])
    xa = [move(b1(1), xp.at[0], "x+"), move(b1(-1), xp.at[1], "x-")]

    for k in (2, 1):
        for c in za:
            c.wait_recv()
        plus4(a1(k), zp.at[2 - k, 0])
        plus4(a1(-k), zp.at[2 - k, 1])
        za = [move(a1(k), zp.at[3 - k, 0], "z+"), move(a1(-k), zp.at[3 - k, 1], "z-")]

    for c in xa:
        c.wait_recv()
    plus(b1(0), xp.at[0], xp.at[1])
    zb = [move(b2(4).at[0], bp0.at[0], "z+"), move(b2(4).at[1], bp0.at[1], "z-")]

    for c in za:
        c.wait_recv()
    plus4(a1(0), zp.at[2, 0], zp.at[2, 1])
    xb = [move(a2(2).at[0], ap0.at[0], "x+"), move(a2(2).at[1], ap0.at[1], "x-")]

    for c in zb:
        c.wait_recv()
    plus1(b2(3).at[0], bp0.at[0])
    plus1(b2(-3).at[1], bp0.at[1])
    zb = [move(b2(3), bp.at[0, 0], "z+"), move(b2(-3), bp.at[0, 1], "z-")]

    for c in xb:
        c.wait_recv()
    plus1(a2(1).at[0], ap0.at[0])
    plus1(a2(-1).at[1], ap0.at[1])
    xb = [move(a2(1), ap.at[0], "x+"), move(a2(-1), ap.at[1], "x-")]

    for k in (2, 1):
        for c in zb:
            c.wait_recv()
        plus(b2(k), bp.at[2 - k, 0])
        plus(b2(-k), bp.at[2 - k, 1])
        zb = [move(b2(k), bp.at[3 - k, 0], "z+"), move(b2(-k), bp.at[3 - k, 1], "z-")]
    for c in xb:
        c.wait_recv()
    plus(a2(0), ap.at[0], ap.at[1])
    ya = [move(acc.at[1 - yl, xh, :, z, 0, xl], yb.at[0], "y")]
    for c in zb:
        c.wait_recv()
    plus(b2(0), bp.at[2, 0], bp.at[2, 1])
    ya.append(move(acc.at[1 - yl, xh, :, z, 1, xl], yb.at[1], "y"))
    for c in range(2):
        ya[c].wait_recv()
        for s in range(3):
            ob[core, s, z, c, xl] = (acc[yl, xh, s, z, c, xl].astype(F32) + yb[c, s].astype(F32)).astype(BF)

    def both_cores(at):
        return move(at, at, "core")

    mine = ob.at[core, :, z, :, xl]
    pair = move(mine, mine, "xs")
    pair.wait_recv()
    chunk = lambda d: ob.at[core, :, zat(d)]
    last = [both_cores(chunk(0))]
    out = [move(chunk(0), chunk(0), "z+"), move(chunk(0), chunk(0), "z-")]
    for k in (1, 2):
        for c in out:
            c.wait_recv()
        out = [move(chunk(-k), chunk(-k), "z+"), move(chunk(k), chunk(k), "z-")]
        last += [both_cores(chunk(-k)), both_cores(chunk(k))]
    for c in out:
        c.wait_recv()
    out = [
        move(chunk(-3).at[:, 0], chunk(-3).at[:, 0], "z+"),
        move(chunk(3).at[:, 1], chunk(3).at[:, 1], "z-"),
    ]
    last += [both_cores(chunk(-3)), both_cores(chunk(3))]
    for c in out:
        c.wait_recv()
    last += [both_cores(chunk(4))]
    for c in last:
        c.wait_recv()
    for c in sends:
        c.wait_send()
    done = pltpu.make_async_copy(ob, o_ref, local.at[0])
    done.start()
    done.wait()


def sum_up(grads):
    n = 64
    lead = (16, CH)
    shape = lambda *d: pltpu.VMEM(d + lead, BF)
    return pl.pallas_call(
        sum_kernel,
        out_shape=jax.ShapeDtypeStruct((2, 3, 8, 2, 2, 16, CH), BF),
        in_specs=[pl.BlockSpec(memory_space=pl.ANY)],
        out_specs=pl.BlockSpec(memory_space=pl.ANY),
        scratch_shapes=[
            shape(2, 2, 3, 8, 2, 2),
            shape(2, 2, 3, 8, 2, 2),
            shape(2, 2, 2, 3),
            shape(3, 2, 2, 2, 3, 2),
            shape(2, 3, 8),
            shape(2, 2, 3, 8),
            shape(2, 3),
            shape(2, 2, 3),
            shape(2, 3),
            shape(3, 2, 2, 3),
            shape(2, 3),
            shape(2, 3, 8, 2, 2),
            pltpu.SemaphoreType.DMA((n,)),
            pltpu.SemaphoreType.DMA((n,)),
            pltpu.SemaphoreType.DMA((1,)),
        ],
        compiler_params=pltpu.CompilerParams(collective_id=3, has_side_effects=True, vmem_limit_bytes=48 << 20),
        name="sum_up",
    )(grads)


def shards(features, labels, classifier, w_mix, w_point, kernels, counts):
    _, _, y, xh, z, xl, core = place()
    stage = y // 2
    image = jnp.where(stage == 0, y, 3 - y) * 2 + xh
    tail = jnp.broadcast_to(counts[0].astype(BF), (3, 7, CH))
    small = jnp.concatenate([kernels, tail], axis=1)
    weights, smalls = gather(w_mix, w_point, small)
    active = (jnp.arange(CELLS) % 3).astype(F32) < smalls[:, 9, 0].astype(F32)
    label = lax.dynamic_index_in_dim(labels, image, 0, keepdims=False)
    flags = jnp.concatenate([active.astype(jnp.int32), jnp.stack([stage, label]).astype(jnp.int32)])
    first = jnp.concatenate([active.astype(jnp.int32), jnp.zeros((2,), jnp.int32)])
    own = lax.dynamic_index_in_dim(features, image, 0, keepdims=False).reshape(GRID, GRID, CH)
    own = jnp.pad(own, ((0, 0), (0, PITCH - GRID), (0, 0))).reshape(ROWS, CH)
    classes = jnp.pad(classifier.T, ((0, 4), (0, 0)))

    (half,) = forward(first, own, jnp.zeros((2, ROWS, CH), BF), weights, smalls, None, False)
    arrived = hop(half)
    _, *saved, head = forward(flags, own, arrived, weights, smalls, classes, True)
    (back,) = backward(flags, head, head, weights, smalls, saved, False)
    arrived = hop(back)
    grads, kernel_grads, _ = backward(flags, arrived, head, weights, smalls, saved, True)
    summed = sum_up(grads.reshape(2, 2, 2, 3, 8, 2, 2, 16, CH))
    summed = summed.reshape(2, 3, CH, CH).astype(F32)

    mine = kernel_grads[:, :9]
    wide = jnp.zeros((2, CELLS, 9, CH), F32)
    wide = lax.dynamic_update_index_in_dim(wide, mine, stage, 0).reshape(24, 9, CH)
    wide = lax.psum(wide, ("segment", "dp"))
    tap = lax.dynamic_slice_in_dim(wide, (y * 2 + xh) * 3, 3, 0)
    return summed[0], summed[1], tap


def solution(mesh):
    return jax.shard_map(
        shards,
        mesh=mesh,
        in_specs=(
            P("dp", None, None),
            P("dp"),
            P(),
            P("segment", None, None),
            P("segment", None, None),
            P("segment", None, None),
            P("segment"),
        ),
        out_specs=(P("segment", None, None), P("segment", None, None), P("segment", None, None)),
        check_vma=False,
    )
```

```python
import functools

import jax
import jax.numpy as jnp
from jax import lax
from jax.experimental import pallas as pl
from jax.experimental.pallas import tpu as pltpu
from jax.sharding import PartitionSpec as P

GRID = 12
PITCH = 16
ROWS = GRID * PITCH
CH = 512
CELLS = 12
EPSILON = 1e-06
MESH = pl.DeviceIdType.MESH
BF = jnp.bfloat16
F32 = jnp.float32


def place():
    seg, dp = lax.axis_index("segment"), lax.axis_index("dp")
    y, xh = seg // 2, seg % 2
    core, xl, z = dp % 2, (dp // 2) % 2, dp // 4
    return seg, dp, y, xh, z, xl, core


def dev(y, xh, z, xl, core):
    return (y * 2 + xh, (z * 2 + xl) * 2 + core)


def neighbours():
    seg, dp, y, xh, z, xl, core = place()
    yp = y + 1 - 2 * (y % 2)
    return {
        "core": dev(y, xh, z, xl, 1 - core),
        "xs": dev(y, xh, z, 1 - xl, core),
        "xd": dev(y, 1 - xh, z, 1 - xl, core),
        "x+": dev(y, jnp.where(xl == 0, xh, 1 - xh), z, 1 - xl, core),
        "x-": dev(y, jnp.where(xl == 1, xh, 1 - xh), z, 1 - xl, core),
        "z+": dev(y, xh, (z + 1) % 8, xl, core),
        "z-": dev(y, xh, (z + 7) % 8, xl, core),
        "y": dev(yp, xh, z, xl, core),
        "hop": dev(3 - y, xh, z, xl, core),
    }


def greet(names, near):
    barrier = pltpu.get_barrier_semaphore()
    for name in names:
        pl.semaphore_signal(barrier, inc=1, device_id=near[name], device_id_type=MESH)
    pl.semaphore_wait(barrier, len(names))


def remote(src, dst, send, recv, i, target):
    return pltpu.make_async_remote_copy(
        src_ref=src, dst_ref=dst, send_sem=send.at[i], recv_sem=recv.at[i], device_id=target, device_id_type=MESH
    )


def gather_kernel(mix_ref, point_ref, small_ref, w_ref, s_ref, send, recv, local):
    _, _, y, xh, z, xl, core = place()
    near = neighbours()
    yl, zp = y % 2, z % 2
    own = yl * 2 + xh
    sec_y, sec_x, sec_xy = (1 - yl) * 2 + xh, yl * 2 + (1 - xh), (1 - yl) * 2 + (1 - xh)
    loc = [
        pltpu.make_async_copy(mix_ref, w_ref.at[0, pl.ds(own * 3, 3)], local.at[0]),
        pltpu.make_async_copy(point_ref, w_ref.at[1, pl.ds(own * 3, 3)], local.at[1]),
        pltpu.make_async_copy(small_ref, s_ref.at[pl.ds(own * 3, 3)], local.at[2]),
    ]
    for c in loc:
        c.start()
    greet(("core", "xs", "xd", "z+", "z-", "y"), near)
    for c in loc:
        c.wait()

    made = []

    def go(sec, slot, row, count, name):
        at = w_ref.at[core, sec * 3 + slot, pl.ds(pl.multiple_of(row, 16), count)]
        c = remote(at, at, send, recv, len(made), near[name])
        made.append(c)
        c.start()
        return c

    def tiny(sec, name):
        at = s_ref.at[pl.ds(sec * 3, 3)]
        c = remote(at, at, send, recv, len(made), near[name])
        made.append(c)
        c.start()
        return c

    mine, other = 128 * (2 * zp + xl), 128 * (2 * zp + 1 - xl)

    def to_z(sec, slot, row):
        return [go(sec, slot, row, 64, "z+"), go(sec, slot, row + 64, 64, "z-")]

    t_y, t_x = tiny(own, "y"), tiny(own, "xd")
    x1, ya, yb, x2, xy1, xy2, zx, zy, zxy, twin = [], [], [], [], [], [], [], [], [], []
    for s in range(3):
        x1.append(go(own, s, other, 128, "xd"))
        ya.append(go(own, s, other, 128, "y"))
    for s in range(3):
        yb.append(go(own, s, mine, 128, "y"))
    t_y.wait_recv()
    t_xy = tiny(sec_y, "xd")
    for s in range(3):
        x1[s].wait_recv()
        x2.append(go(sec_x, s, mine, 128, "xs"))
        zx.append(to_z(sec_x, s, mine))
        ya[s].wait_recv()
        xy1.append(go(sec_y, s, other, 128, "xd"))
        zy.append(to_z(sec_y, s, other))
    for s in range(3):
        x2[s].wait_recv()
        zx[s] += to_z(sec_x, s, other)
        twin.append(go(sec_x, s, 256 * zp, 256, "core"))
    for s in range(3):
        xy1[s].wait_recv()
        xy2.append(go(sec_xy, s, mine, 128, "xs"))
        zxy.append(to_z(sec_xy, s, mine))
        yb[s].wait_recv()
        zy[s] += to_z(sec_y, s, mine)
        twin.append(go(sec_y, s, 256 * zp, 256, "core"))
    for s in range(3):
        xy2[s].wait_recv()
        zxy[s] += to_z(sec_xy, s, other)
        twin.append(go(sec_xy, s, 256 * zp, 256, "core"))
    for sec, group in ((sec_x, zx), (sec_y, zy), (sec_xy, zxy)):
        for s in range(3):
            for c in group[s]:
                c.wait_recv()
            twin.append(go(sec, s, 256 * (1 - zp), 256, "core"))
    for c in twin + [t_x, t_xy]:
        c.wait_recv()
    for c in made:
        c.wait_send()


def gather(w_mix, w_point, small):
    return pl.pallas_call(
        gather_kernel,
        out_shape=(
            jax.ShapeDtypeStruct((2, CELLS, CH, CH), BF),
            jax.ShapeDtypeStruct((CELLS, 16, CH), BF),
        ),
        in_specs=[pl.BlockSpec(memory_space=pl.ANY)] * 3,
        out_specs=(pl.BlockSpec(memory_space=pltpu.VMEM),) * 2,
        scratch_shapes=[
            pltpu.SemaphoreType.DMA((75,)),
            pltpu.SemaphoreType.DMA((75,)),
            pltpu.SemaphoreType.DMA((3,)),
        ],
        compiler_params=pltpu.CompilerParams(collective_id=1, has_side_effects=True, vmem_limit_bytes=40 << 20),
        name="gather",
    )(w_mix, w_point, small)


def hop_kernel(x_ref, o_ref, send, recv):
    near = neighbours()
    greet(("hop",), near)
    copies = [remote(x_ref.at[i], o_ref.at[i], send, recv, i, near["hop"]) for i in range(2)]
    for c in copies:
        c.start()
    for c in copies:
        c.wait()


def hop(x):
    return pl.pallas_call(
        hop_kernel,
        out_shape=jax.ShapeDtypeStruct(x.shape, x.dtype),
        in_specs=[pl.BlockSpec(memory_space=pl.ANY)],
        out_specs=pl.BlockSpec(memory_space=pl.ANY),
        scratch_shapes=[pltpu.SemaphoreType.DMA((2,)), pltpu.SemaphoreType.DMA((2,))],
        compiler_params=pltpu.CompilerParams(collective_id=2, has_side_effects=True),
        name="hop",
    )(x)


def down(r):
    return jnp.concatenate([jnp.zeros((PITCH, r.shape[1]), r.dtype), r[:-PITCH]], axis=0)


def up(r):
    return jnp.concatenate([r[PITCH:], jnp.zeros((PITCH, r.shape[1]), r.dtype)], axis=0)


def fwd_kernel(save, flags, xa_ref, xb_ref, w_ref, k_ref, *rest):
    if save:
        c_ref, o_ref, sp_ref, so_ref, ss_ref, st_ref, hg_ref, sep = rest
    else:
        o_ref, sep = rest
    i = pl.program_id(0)

    @pl.when(i == 0)
    def _():
        @pl.when(flags[CELLS] == 0)
        def _():
            o_ref[0] = xa_ref[...]
            o_ref[1] = xa_ref[...]

        @pl.when(flags[CELLS] != 0)
        def _():
            o_ref[...] = xb_ref[...]

    @pl.when(flags[i] == 1)
    def _():
        if save:
            sp_ref[0] = o_ref[0]
            so_ref[0] = o_ref[1]
        real = lax.broadcasted_iota(jnp.int32, (ROWS, 128), 0) % PITCH < GRID
        for c in range(4):
            cols = slice(128 * c, 128 * c + 128)
            a = jnp.maximum(o_ref[1, :, cols].astype(F32), 0.0)
            k = k_ref[0, :, cols].astype(F32)
            am, ap = pltpu.roll(a, 1, 0), pltpu.roll(a, ROWS - 1, 0)
            r = [k[3 * u : 3 * u + 1] * am + k[3 * u + 1 : 3 * u + 2] * a + k[3 * u + 2 : 3 * u + 3] * ap for u in range(3)]
            s = r[1] + down(r[0]) + up(r[2])
            sep[:, cols] = jnp.where(real, s, 0.0).astype(BF)
        if save:
            ss_ref[0] = sep[...]
        prev = o_ref[0]
        total = jnp.dot(sep[...], w_ref[1, 0], preferred_element_type=F32)
        total = total + jnp.dot(jnp.maximum(prev, 0), w_ref[0, 0], preferred_element_type=F32)
        total = prev.astype(F32) + total
        q = lax.rsqrt(jnp.mean(total * total, axis=-1, keepdims=True) + EPSILON)
        if save:
            st_ref[0] = total
        o_ref[1] = prev
        o_ref[0] = (total * q).astype(BF)

    if save:

        @pl.when(i == CELLS - 1)
        def _():
            last = o_ref[0]
            pooled = jnp.sum(jnp.maximum(last.astype(F32), 0.0), axis=0, keepdims=True) / (GRID * GRID)
            grad = jnp.zeros((1, CH), F32)
            for k in range(4):
                row = c_ref[k : k + 1, :]
                logit = jnp.sum(pooled * row, axis=-1, keepdims=True)
                hot = jnp.where(flags[CELLS + 1] == k, 1.0, 0.0)
                grad = grad + (logit - hot) * row
            grad = grad / (GRID * GRID)
            hg_ref[0] = jnp.where(last > 0, jnp.broadcast_to(grad, last.shape), 0.0).astype(BF)
            hg_ref[1] = jnp.zeros((ROWS, CH), BF)


def forward(flags, image, arrived, weights, small, classes, save):
    whole = lambda n: pl.BlockSpec(n, lambda i, f: (0,) * len(n))
    one = lambda n: pl.BlockSpec((1,) + n, lambda i, f: (i, 0, 0))
    pair = jax.ShapeDtypeStruct((2, ROWS, CH), BF)
    in_specs = [
        whole((ROWS, CH)),
        whole((2, ROWS, CH)),
        pl.BlockSpec((2, 1, CH, CH), lambda i, f: (0, i, 0, 0)),
        one((16, CH)),
    ]
    out_specs, out_shape = [whole((2, ROWS, CH))], [pair]
    args = [flags, image, arrived, weights, small]
    if save:
        in_specs.append(whole((8, CH)))
        args.append(classes)
        out_specs += [one((ROWS, CH))] * 4 + [whole((2, ROWS, CH))]
        kept = jax.ShapeDtypeStruct((CELLS, ROWS, CH), BF)
        out_shape += [kept, kept, kept, jax.ShapeDtypeStruct((CELLS, ROWS, CH), F32), pair]
    return pl.pallas_call(
        functools.partial(fwd_kernel, save),
        grid_spec=pltpu.PrefetchScalarGridSpec(
            num_scalar_prefetch=1,
            grid=(CELLS,),
            in_specs=in_specs,
            out_specs=out_specs,
            scratch_shapes=[pltpu.VMEM((ROWS, CH), BF)],
        ),
        out_shape=out_shape,
        compiler_params=pltpu.CompilerParams(vmem_limit_bytes=56 << 20),
        name="forward_save" if save else "forward",
    )(*args)


NT = (((1,), (1,)), ((), ()))
TN = (((0,), (0,)), ((), ()))


def bwd_kernel(wgrad, flags, ga_ref, gb_ref, w_ref, k_ref, sp_ref, so_ref, ss_ref, st_ref, *rest):
    if wgrad:
        gw_ref, gk_ref, o_ref, gs, taps = rest
    else:
        o_ref, gs, taps = rest
    i = pl.program_id(0)
    cell = CELLS - 1 - i

    @pl.when(i == 0)
    def _():
        @pl.when(flags[CELLS] == 0)
        def _():
            o_ref[...] = ga_ref[...]

        @pl.when(flags[CELLS] != 0)
        def _():
            o_ref[...] = gb_ref[...]

    @pl.when(flags[cell] == 1)
    def _():
        total = st_ref[0]
        q = lax.rsqrt(jnp.mean(total * total, axis=-1, keepdims=True) + EPSILON)
        n = total * q
        gn = o_ref[0].astype(F32)
        gt = q * (gn - n * jnp.mean(gn * n, axis=-1, keepdims=True))
        gh = gt.astype(BF)
        gs[...] = lax.dot_general(gh, w_ref[1, 0], NT, preferred_element_type=F32)
        gm = lax.dot_general(gh, w_ref[0, 0], NT, preferred_element_type=F32)
        prev = sp_ref[0]
        o_ref[0] = (gt + jnp.where(prev > 0, gm, 0.0) + o_ref[1].astype(F32)).astype(BF)
        for c in range(4):
            cols = slice(128 * c, 128 * c + 128)
            g = gs[:, cols]
            k = k_ref[0, :, cols].astype(F32)
            gv = [pltpu.roll(g, ROWS - 1, 0), g, pltpu.roll(g, 1, 0)]
            r = [
                k[3 * u : 3 * u + 1] * gv[0] + k[3 * u + 1 : 3 * u + 2] * gv[1] + k[3 * u + 2 : 3 * u + 3] * gv[2]
                for u in range(3)
            ]
            rel = r[1] + up(r[0]) + down(r[2])
            older = so_ref[0, :, cols]
            o_ref[1, :, cols] = jnp.where(older > 0, rel, 0.0).astype(BF)
            if wgrad:
                a = jnp.maximum(older.astype(F32), 0.0)
                for v in range(3):
                    taps[v : v + 1, cols] = jnp.sum(a[:-PITCH] * gv[v][PITCH:], axis=0, keepdims=True)
                    taps[3 + v : 4 + v, cols] = jnp.sum(a * gv[v], axis=0, keepdims=True)
                    taps[6 + v : 7 + v, cols] = jnp.sum(a[PITCH:] * gv[v][:-PITCH], axis=0, keepdims=True)
        if wgrad:
            gk_ref[0] = taps[...].astype(BF)
            gw_ref[0, 0] = lax.dot_general(jnp.maximum(prev, 0), gh, TN, preferred_element_type=F32).astype(BF)
            gw_ref[1, 0] = lax.dot_general(ss_ref[0], gh, TN, preferred_element_type=F32).astype(BF)

    if wgrad:

        @pl.when(flags[cell] != 1)
        def _():
            gw_ref[...] = jnp.zeros_like(gw_ref)
            gk_ref[...] = jnp.zeros_like(gk_ref)


def backward(flags, arrived, head, weights, small, saved, wgrad):
    whole = lambda n: pl.BlockSpec(n, lambda i, f: (0,) * len(n))
    one = lambda n: pl.BlockSpec((1,) + n, lambda i, f: (CELLS - 1 - i, 0, 0))
    both = pl.BlockSpec((2, 1, CH, CH), lambda i, f: (0, CELLS - 1 - i, 0, 0))
    out_specs, out_shape = [whole((2, ROWS, CH))], [jax.ShapeDtypeStruct((2, ROWS, CH), BF)]
    if wgrad:
        out_specs = [both, one((16, CH))] + out_specs
        out_shape = [
            jax.ShapeDtypeStruct((2, CELLS, CH, CH), BF),
            jax.ShapeDtypeStruct((CELLS, 16, CH), BF),
        ] + out_shape
    return pl.pallas_call(
        functools.partial(bwd_kernel, wgrad),
        grid_spec=pltpu.PrefetchScalarGridSpec(
            num_scalar_prefetch=1,
            grid=(CELLS,),
            in_specs=[whole((2, ROWS, CH)), whole((2, ROWS, CH)), both, one((16, CH))] + [one((ROWS, CH))] * 4,
            out_specs=out_specs,
            scratch_shapes=[pltpu.VMEM((ROWS, CH), F32), pltpu.VMEM((16, CH), F32)],
        ),
        out_shape=out_shape,
        compiler_params=pltpu.CompilerParams(vmem_limit_bytes=56 << 20),
        name="backward_weights" if wgrad else "backward",
    )(flags, arrived, head, weights, small, *saved)


def sum_kernel(g_ref, k_ref, o_ref, t_ref, tk, tr, ty, tx, tz, acc, rb, zp0, zp, xp0, xp, ap0, ap, bp0, bp, yb, ob, send, recv, local):
    _, _, y, xh, z, xl, core = place()
    near = neighbours()
    yl = y % 2
    count = [0]
    sends = []

    def move(src, dst, name):
        c = remote(src, dst, send, recv, count[0], near[name])
        count[0] += 1
        sends.append(c)
        c.start()
        return c

    load = pltpu.make_async_copy(g_ref.at[core], acc, local.at[0])
    load.start()
    load_taps = pltpu.make_async_copy(k_ref, tk, local.at[1])
    load_taps.start()
    greet(("core", "xs", "xd", "z+", "z-", "y"), near)
    load_taps.wait()
    step = move(tk, tr, "core")
    twin = [move(g_ref.at[1 - core, a, b], rb.at[a, b], "core") for a in range(2) for b in range(2)]
    load.wait()
    for j in range(4):
        a, b = j // 2, j % 2
        twin[j].wait_recv()

        def add(n, _, a=a, b=b):
            s, zz = n // 8, n % 8
            acc[a, b, s, zz] = (acc[a, b, s, zz].astype(F32) + rb[a, b, s, zz].astype(F32)).astype(BF)
            return 0

        lax.fori_loop(0, 24, add, 0)

    def plus(ref, *others):
        def step(s, _):
            v = ref[:, s].astype(F32)
            for o in others:
                v = v + o[:, s].astype(F32)
            ref[:, s] = v.astype(BF)
            return 0

        lax.fori_loop(0, 3, step, 0)

    def zat(d):
        return (z + 8 + d) % 8

    def xat(d):
        x = (xh * 2 + xl + 4 + d) % 4
        return x // 2, x % 2

    def a1(d):
        return acc.at[:, :, :, zat(d), 0]

    def b1(d):
        h, l = xat(d)
        return acc.at[:, h, :, :, 1, l]

    def a2(d):
        h, l = xat(d)
        return acc.at[:, h, :, z, 0, l]

    def b2(d):
        return acc.at[:, xh, :, zat(d), 1, xl]

    def plus4(ref, *others):
        def step(n, _):
            a, b = n // 2, n % 2
            v = ref[a, b].astype(F32)
            for o in others:
                v = v + o[a, b].astype(F32)
            ref[a, b] = v.astype(BF)
            return 0

        lax.fori_loop(0, 4, step, 0)

    def fold(dst, a, b):
        for s in range(3):
            dst[s] = (a[s].astype(F32) + b[s].astype(F32)).astype(BF)

    step.wait_recv()
    for a in range(2):
        for b in range(2):
            fold(tr.at[a, b], tr.at[a, b], tk.at[a, b])
    step = move(tr.at[1 - yl], ty, "y")

    za = [move(a1(4).at[:, :, :, 0], zp0.at[0], "z+"), move(a1(4).at[:, :, :, 1], zp0.at[1], "z-")]
    xa = [move(b1(2).at[0], xp0.at[0], "x+"), move(b1(2).at[1], xp0.at[1], "x-")]

    for c in za:
        c.wait_recv()
    plus4(a1(3).at[:, :, :, 0], zp0.at[0])
    plus4(a1(-3).at[:, :, :, 1], zp0.at[1])
    za = [move(a1(3), zp.at[0, 0], "z+"), move(a1(-3), zp.at[0, 1], "z-")]
    step.wait_recv()
    for b in range(2):
        fold(ty.at[b], ty.at[b], tr.at[yl, b])
    step = move(ty.at[1 - xh], tx.at[0], "xd")

    for c in xa:
        c.wait_recv()

    def plus1(ref, other):
        def step(s, _):
            ref[s] = (ref[s].astype(F32) + other[s].astype(F32)).astype(BF)
            return 0

        lax.fori_loop(0, 3, step, 0)

    plus1(b1(1).at[0], xp0.at[0])
    plus1(b1(-1).at[1], xp0.at[1])
    xa = [move(b1(1), xp.at[0], "x+"), move(b1(-1), xp.at[1], "x-")]

    step.wait_recv()
    fold(tx.at[0], tx.at[0], ty.at[xh])
    step = move(tx.at[0], tx.at[1], "xs")

    for k in (2, 1):
        for c in za:
            c.wait_recv()
        plus4(a1(k), zp.at[2 - k, 0])
        plus4(a1(-k), zp.at[2 - k, 1])
        za = [move(a1(k), zp.at[3 - k, 0], "z+"), move(a1(-k), zp.at[3 - k, 1], "z-")]

    step.wait_recv()
    fold(tz.at[0, 0], tx.at[0], tx.at[1])
    step = [move(tz.at[0, 0], tz.at[1, 0], "z+"), move(tz.at[0, 0], tz.at[1, 1], "z-")]

    for c in xa:
        c.wait_recv()
    plus(b1(0), xp.at[0], xp.at[1])
    zb = [move(b2(4).at[0], bp0.at[0], "z+"), move(b2(4).at[1], bp0.at[1], "z-")]

    for c in za:
        c.wait_recv()
    plus4(a1(0), zp.at[2, 0], zp.at[2, 1])
    xb = [move(a2(2).at[0], ap0.at[0], "x+"), move(a2(2).at[1], ap0.at[1], "x-")]

    for c in zb:
        c.wait_recv()
    plus1(b2(3).at[0], bp0.at[0])
    plus1(b2(-3).at[1], bp0.at[1])
    zb = [move(b2(3), bp.at[0, 0], "z+"), move(b2(-3), bp.at[0, 1], "z-")]

    for c in xb:
        c.wait_recv()
    plus1(a2(1).at[0], ap0.at[0])
    plus1(a2(-1).at[1], ap0.at[1])
    xb = [move(a2(1), ap.at[0], "x+"), move(a2(-1), ap.at[1], "x-")]

    for k in (2, 1):
        for c in step:
            c.wait_recv()
        step = [move(tz.at[3 - k, 0], tz.at[4 - k, 0], "z+"), move(tz.at[3 - k, 1], tz.at[4 - k, 1], "z-")]
        for c in zb:
            c.wait_recv()
        plus(b2(k), bp.at[2 - k, 0])
        plus(b2(-k), bp.at[2 - k, 1])
        zb = [move(b2(k), bp.at[3 - k, 0], "z+"), move(b2(-k), bp.at[3 - k, 1], "z-")]
    for c in xb:
        c.wait_recv()
    plus(a2(0), ap.at[0], ap.at[1])
    ya = [move(acc.at[1 - yl, xh, :, z, 0, xl], yb.at[0], "y")]
    for c in zb:
        c.wait_recv()
    plus(b2(0), bp.at[2, 0], bp.at[2, 1])
    ya.append(move(acc.at[1 - yl, xh, :, z, 1, xl], yb.at[1], "y"))
    for c in range(2):
        ya[c].wait_recv()
        for s in range(3):
            ob[core, s, z, c, xl] = (acc[yl, xh, s, z, c, xl].astype(F32) + yb[c, s].astype(F32)).astype(BF)

    for c in step:
        c.wait_recv()
    step = move(tz.at[3, 0], tz.at[4, 0], "z+")

    def both_cores(at):
        return move(at, at, "core")

    mine = ob.at[core, :, z, :, xl]
    pair = move(mine, mine, "xs")
    pair.wait_recv()
    chunk = lambda d: ob.at[core, :, zat(d)]
    last = [both_cores(chunk(0))]
    out = [move(chunk(0), chunk(0), "z+"), move(chunk(0), chunk(0), "z-")]
    for k in (1, 2):
        for c in out:
            c.wait_recv()
        out = [move(chunk(-k), chunk(-k), "z+"), move(chunk(k), chunk(k), "z-")]
        last += [both_cores(chunk(-k)), both_cores(chunk(k))]
    for c in out:
        c.wait_recv()
    out = [
        move(chunk(-3).at[:, 0], chunk(-3).at[:, 0], "z+"),
        move(chunk(3).at[:, 1], chunk(3).at[:, 1], "z-"),
    ]
    last += [both_cores(chunk(-3)), both_cores(chunk(3))]
    for c in out:
        c.wait_recv()
    last += [both_cores(chunk(4))]
    for c in last:
        c.wait_recv()
    for c in sends:
        c.wait_send()
    done = pltpu.make_async_copy(ob, o_ref, local.at[0])
    done.start()
    step.wait_recv()
    for s in range(3):
        v = tz[0, 0, s].astype(F32) + tz[4, 0, s].astype(F32)
        for k in (1, 2, 3):
            v = v + tz[k, 0, s].astype(F32) + tz[k, 1, s].astype(F32)
        t_ref[s] = v
    done.wait()


def sum_up(grads, taps):
    n = 80
    lead = (16, CH)
    shape = lambda *d: pltpu.VMEM(d + lead, BF)
    return pl.pallas_call(
        sum_kernel,
        out_shape=(jax.ShapeDtypeStruct((2, 3, 8, 2, 2, 16, CH), BF), jax.ShapeDtypeStruct((3, 16, CH), F32)),
        in_specs=[pl.BlockSpec(memory_space=pl.ANY)] * 2,
        out_specs=(pl.BlockSpec(memory_space=pl.ANY), pl.BlockSpec(memory_space=pltpu.VMEM)),
        scratch_shapes=[
            shape(2, 2, 3),
            shape(2, 2, 3),
            shape(2, 3),
            shape(2, 3),
            shape(5, 2, 3),
            shape(2, 2, 3, 8, 2, 2),
            shape(2, 2, 3, 8, 2, 2),
            shape(2, 2, 2, 3),
            shape(3, 2, 2, 2, 3, 2),
            shape(2, 3, 8),
            shape(2, 2, 3, 8),
            shape(2, 3),
            shape(2, 2, 3),
            shape(2, 3),
            shape(3, 2, 2, 3),
            shape(2, 3),
            shape(2, 3, 8, 2, 2),
            pltpu.SemaphoreType.DMA((n,)),
            pltpu.SemaphoreType.DMA((n,)),
            pltpu.SemaphoreType.DMA((2,)),
        ],
        compiler_params=pltpu.CompilerParams(collective_id=3, has_side_effects=True, vmem_limit_bytes=48 << 20),
        name="sum_up",
    )(grads, taps)


def shards(features, labels, classifier, w_mix, w_point, kernels, counts):
    _, _, y, xh, z, xl, core = place()
    stage = y // 2
    image = jnp.where(stage == 0, y, 3 - y) * 2 + xh
    tail = jnp.broadcast_to(counts[0].astype(BF), (3, 7, CH))
    small = jnp.concatenate([kernels, tail], axis=1)
    weights, smalls = gather(w_mix, w_point, small)
    active = (jnp.arange(CELLS) % 3).astype(F32) < smalls[:, 9, 0].astype(F32)
    label = lax.dynamic_index_in_dim(labels, image, 0, keepdims=False)
    flags = jnp.concatenate([active.astype(jnp.int32), jnp.stack([stage, label]).astype(jnp.int32)])
    first = jnp.concatenate([active.astype(jnp.int32), jnp.zeros((2,), jnp.int32)])
    own = lax.dynamic_index_in_dim(features, image, 0, keepdims=False).reshape(GRID, GRID, CH)
    own = jnp.pad(own, ((0, 0), (0, PITCH - GRID), (0, 0))).reshape(ROWS, CH)
    classes = jnp.pad(classifier.T, ((0, 4), (0, 0)))

    (half,) = forward(first, own, jnp.zeros((2, ROWS, CH), BF), weights, smalls, None, False)
    arrived = hop(half)
    _, *saved, head = forward(flags, own, arrived, weights, smalls, classes, True)
    (back,) = backward(flags, head, head, weights, smalls, saved, False)
    arrived = hop(back)
    grads, kernel_grads, _ = backward(flags, arrived, head, weights, smalls, saved, True)
    summed, taps = sum_up(grads.reshape(2, 2, 2, 3, 8, 2, 2, 16, CH), kernel_grads.reshape(2, 2, 3, 16, CH))
    summed = summed.reshape(2, 3, CH, CH).astype(F32)
    return summed[0], summed[1], taps[:, :9]


def solution(mesh):
    return jax.shard_map(
        shards,
        mesh=mesh,
        in_specs=(
            P("dp", None, None),
            P("dp"),
            P(),
            P("segment", None, None),
            P("segment", None, None),
            P("segment", None, None),
            P("segment"),
        ),
        out_specs=(P("segment", None, None), P("segment", None, None), P("segment", None, None)),
        check_vma=False,
    )
```

```python
import jax
import jax.numpy as jnp
from jax import lax
from jax.experimental import pallas as pl
from jax.experimental.pallas import tpu as pltpu
from jax.sharding import PartitionSpec as P

GRID = 12
PITCH = 16
ROWS = GRID * PITCH
CH = 512
CELLS = 12
EPSILON = 1e-06
MESH = pl.DeviceIdType.MESH
BF = jnp.bfloat16
F32 = jnp.float32


def place():
    seg, dp = lax.axis_index("segment"), lax.axis_index("dp")
    y, xh = seg // 2, seg % 2
    core, xl, z = dp % 2, (dp // 2) % 2, dp // 4
    return seg, dp, y, xh, z, xl, core


def dev(y, xh, z, xl, core):
    return (y * 2 + xh, (z * 2 + xl) * 2 + core)


def neighbours():
    seg, dp, y, xh, z, xl, core = place()
    yp = y + 1 - 2 * (y % 2)
    return {
        "core": dev(y, xh, z, xl, 1 - core),
        "xs": dev(y, xh, z, 1 - xl, core),
        "xd": dev(y, 1 - xh, z, 1 - xl, core),
        "x+": dev(y, jnp.where(xl == 0, xh, 1 - xh), z, 1 - xl, core),
        "x-": dev(y, jnp.where(xl == 1, xh, 1 - xh), z, 1 - xl, core),
        "z+": dev(y, xh, (z + 1) % 8, xl, core),
        "z-": dev(y, xh, (z + 7) % 8, xl, core),
        "y": dev(yp, xh, z, xl, core),
        "hop": dev(3 - y, xh, z, xl, core),
    }


def greet(names, near):
    barrier = pltpu.get_barrier_semaphore()
    for name in names:
        pl.semaphore_signal(barrier, inc=1, device_id=near[name], device_id_type=MESH)
    pl.semaphore_wait(barrier, len(names))


def remote(src, dst, send, recv, i, target):
    return pltpu.make_async_remote_copy(
        src_ref=src, dst_ref=dst, send_sem=send.at[i], recv_sem=recv.at[i], device_id=target, device_id_type=MESH
    )


def down(r):
    return jnp.concatenate([jnp.zeros((PITCH, r.shape[1]), r.dtype), r[:-PITCH]], axis=0)


def up(r):
    return jnp.concatenate([r[PITCH:], jnp.zeros((PITCH, r.shape[1]), r.dtype)], axis=0)


NT = (((1,), (1,)), ((), ()))
TN = (((0,), (0,)), ((), ()))


def parts_of(cell):
    return cell // 6, (cell // 3) % 2, cell % 3


def kernel(
    f_ref, mix_ref, point_ref, small_ref, class_ref, o_ref, t_ref,
    w_ref, s_ref, img, st, ho, hi, sp, so, ss, tt, gs, taps, gw, rb,
    tk, tr, ty, tx, tz, zp0, zp, xp0, xp, ap0, ap, bp0, bp, yb, ob, send, recv, local,
):
    _, _, y, xh, z, xl, core = place()
    near = neighbours()
    stage, yl, zpar = y // 2, y % 2, z % 2
    image = jnp.where(stage == 0, y, 3 - y) * 2 + xh
    own = yl * 2 + xh
    sec_y, sec_x, sec_xy = (1 - yl) * 2 + xh, yl * 2 + (1 - xh), (1 - yl) * 2 + (1 - xh)
    count = [14]
    sends = []

    def move(src, dst, name):
        c = remote(src, dst, send, recv, count[0], near[name])
        count[0] += 1
        sends.append(c)
        c.start()
        return c

    loc = [
        pltpu.make_async_copy(small_ref, s_ref.at[pl.ds(own * 3, 3)], local.at[2]),
        pltpu.make_async_copy(mix_ref, w_ref.at[0, pl.ds(own * 3, 3)], local.at[0]),
        pltpu.make_async_copy(point_ref, w_ref.at[1, pl.ds(own * 3, 3)], local.at[1]),
        pltpu.make_async_copy(f_ref.at[image], img, local.at[3]),
    ]
    for c in loc:
        c.start()
    greet(("core", "xs", "xd", "z+", "z-", "y", "hop"), near)
    for c in loc:
        c.wait()

    def go(sec, slot, row, count, name):
        at = w_ref.at[core, sec * 3 + slot, pl.ds(pl.multiple_of(row, 16), count)]
        return move(at, at, name)

    def tiny(sec, name):
        at = s_ref.at[pl.ds(sec * 3, 3)]
        return move(at, at, name)

    mine, other = 128 * (2 * zpar + xl), 128 * (2 * zpar + 1 - xl)

    def to_z(sec, slot, row):
        return [go(sec, slot, row, 64, "z+"), go(sec, slot, row + 64, 64, "z-")]

    t_y, t_x = tiny(own, "y"), tiny(own, "xd")
    x1, y_first, y_then, x2, xy1, xy2, zx, zy, zxy, twin = [], [], [], [], [], [], [], [], [], []
    for s in range(3):
        x1.append(go(own, s, other, 128, "xd"))
        y_first.append(go(own, s, other, 128, "y"))
    for s in range(3):
        y_then.append(go(own, s, mine, 128, "y"))
    t_y.wait_recv()
    t_xy = tiny(sec_y, "xd")
    for s in range(3):
        x1[s].wait_recv()
        x2.append(go(sec_x, s, mine, 128, "xs"))
        zx.append(to_z(sec_x, s, mine))
        y_first[s].wait_recv()
        xy1.append(go(sec_y, s, other, 128, "xd"))
        zy.append(to_z(sec_y, s, other))
    for s in range(3):
        x2[s].wait_recv()
        zx[s] += to_z(sec_x, s, other)
        twin.append(go(sec_x, s, 256 * zpar, 256, "core"))
    for s in range(3):
        xy1[s].wait_recv()
        xy2.append(go(sec_xy, s, mine, 128, "xs"))
        zxy.append(to_z(sec_xy, s, mine))
        y_then[s].wait_recv()
        zy[s] += to_z(sec_y, s, mine)
        twin.append(go(sec_y, s, 256 * zpar, 256, "core"))
    for s in range(3):
        xy2[s].wait_recv()
        zxy[s] += to_z(sec_xy, s, other)
        twin.append(go(sec_xy, s, 256 * zpar, 256, "core"))
    for sec, group in ((sec_x, zx), (sec_y, zy), (sec_xy, zxy)):
        for s in range(3):
            for c in group[s]:
                c.wait_recv()
            twin.append(go(sec, s, 256 * (1 - zpar), 256, "core"))

    image_in = img[...].astype(F32)
    for r in range(GRID):
        row = jnp.concatenate([image_in[GRID * r : GRID * r + GRID], jnp.zeros((PITCH - GRID, CH), F32)], axis=0)
        st[0, PITCH * r : PITCH * r + PITCH] = row.astype(BF)
        st[1, PITCH * r : PITCH * r + PITCH] = row.astype(BF)
    for c in twin + [t_x, t_xy]:
        c.wait_recv()

    hops = [remote(ho.at[i], hi.at[i], send, recv, 12 + i, near["hop"]) for i in range(2)]
    real = lax.broadcasted_iota(jnp.int32, (ROWS, 128), 0) % PITCH < GRID

    def holds(cell, cols=slice(None)):
        return s_ref[cell, 9:10, cols].astype(F32) > (cell % 3).astype(F32)

    def cell_forward(cell, _):
        sp[cell] = st[0]
        so[cell] = st[1]
        for c in range(4):
            cols = slice(128 * c, 128 * c + 128)
            a = jnp.maximum(st[1, :, cols].astype(F32), 0.0)
            k = s_ref[cell, :, cols].astype(F32)
            am, ap_ = pltpu.roll(a, 1, 0), pltpu.roll(a, ROWS - 1, 0)
            r = [k[3 * u : 3 * u + 1] * am + k[3 * u + 1 : 3 * u + 2] * a + k[3 * u + 2 : 3 * u + 3] * ap_ for u in range(3)]
            s = r[1] + down(r[0]) + up(r[2])
            ss[cell, :, cols] = jnp.where(real, s, 0.0).astype(BF)
        prev = st[0]
        total = jnp.dot(ss[cell], w_ref[1, cell], preferred_element_type=F32)
        total = total + jnp.dot(jnp.maximum(prev, 0), w_ref[0, cell], preferred_element_type=F32)
        prev = prev.astype(F32)
        total = prev + total
        q = lax.rsqrt(jnp.mean(total * total, axis=-1, keepdims=True) + EPSILON)
        tt[cell] = total
        on = holds(cell)
        st[1] = jnp.where(on, prev, st[1].astype(F32)).astype(BF)
        st[0] = jnp.where(on, total * q, prev).astype(BF)
        return 0

    def head():
        last = st[0].astype(F32)
        pooled = jnp.sum(jnp.maximum(last, 0.0), axis=0, keepdims=True) / (GRID * GRID)
        grad = jnp.zeros((1, CH), F32)
        for k in range(4):
            row = class_ref[0, k : k + 1, :]
            logit = jnp.sum(pooled * row, axis=-1, keepdims=True)
            grad = grad + (logit - class_ref[1, k : k + 1, :]) * row
        grad = grad / (GRID * GRID)
        ho[0] = jnp.where(last > 0, jnp.broadcast_to(grad, last.shape), 0.0).astype(BF)
        ho[1] = jnp.zeros((ROWS, CH), BF)

    def twin_of(cell):
        a, b, s = parts_of(cell)
        return remote(gw.at[1 - core, a, b, s], rb.at[a, b, s], send, recv, cell, near["core"])

    def join(cell):
        a, b, s = parts_of(cell)
        twin_of(cell).wait_recv()
        gw[core, a, b, s] = (gw[core, a, b, s].astype(F32) + rb[a, b, s].astype(F32)).astype(BF)

    def cell_backward(i, g, wgrad):
        cell = CELLS - 1 - i
        a_, b_, s_ = parts_of(cell)
        total = tt[cell]
        q = lax.rsqrt(jnp.mean(total * total, axis=-1, keepdims=True) + EPSILON)
        n = total * q
        gn = g[0].astype(F32)
        on = holds(cell)
        gt = q * (gn - n * jnp.mean(gn * n, axis=-1, keepdims=True))
        gt = jnp.where(on, gt, 0.0)
        gh = gt.astype(BF)
        gs[...] = lax.dot_general(gh, w_ref[1, cell], NT, preferred_element_type=F32)
        gm = lax.dot_general(gh, w_ref[0, cell], NT, preferred_element_type=F32)
        prev = sp[cell]
        g[0] = jnp.where(on, gt + jnp.where(prev > 0, gm, 0.0) + g[1].astype(F32), gn).astype(BF)
        for c in range(4):
            cols = slice(128 * c, 128 * c + 128)
            u_ = gs[:, cols]
            k = s_ref[cell, :, cols].astype(F32)
            gv = [pltpu.roll(u_, ROWS - 1, 0), u_, pltpu.roll(u_, 1, 0)]
            r = [
                k[3 * u : 3 * u + 1] * gv[0] + k[3 * u + 1 : 3 * u + 2] * gv[1] + k[3 * u + 2 : 3 * u + 3] * gv[2]
                for u in range(3)
            ]
            rel = r[1] + up(r[0]) + down(r[2])
            older = so[cell, :, cols].astype(F32)
            g[1, :, cols] = jnp.where(holds(cell, cols), jnp.where(older > 0, rel, 0.0), g[1, :, cols].astype(F32)).astype(BF)
            if wgrad:
                a = jnp.maximum(older, 0.0)
                for v in range(3):
                    taps[v : v + 1, cols] = jnp.sum(a[:-PITCH] * gv[v][PITCH:], axis=0, keepdims=True)
                    taps[3 + v : 4 + v, cols] = jnp.sum(a * gv[v], axis=0, keepdims=True)
                    taps[6 + v : 7 + v, cols] = jnp.sum(a[PITCH:] * gv[v][:-PITCH], axis=0, keepdims=True)
        if wgrad:
            tk[a_, b_, s_] = taps[...].astype(BF)
            parts = (8, 2, 2, 16, CH)
            gw[0, a_, b_, s_] = (
                lax.dot_general(jnp.maximum(prev, 0), gh, TN, preferred_element_type=F32).astype(BF).reshape(parts)
            )
            gw[1, a_, b_, s_] = lax.dot_general(ss[cell], gh, TN, preferred_element_type=F32).astype(BF).reshape(parts)
            twin_of(cell).start()

            @pl.when(i >= 2)
            def _():
                join(cell + 2)

        return 0

    taps[...] = jnp.zeros_like(taps)

    @pl.when(stage == 1)
    def _():
        for c in hops:
            c.wait_recv()
        st[...] = hi[...]

    lax.fori_loop(0, CELLS, cell_forward, 0)

    @pl.when(stage == 0)
    def _():
        ho[...] = st[...]
        for c in hops:
            c.start()
        for c in hops:
            c.wait_recv()

    @pl.when(stage == 1)
    def _():
        head()
        hi[...] = ho[...]
        lax.fori_loop(0, CELLS, lambda i, _: cell_backward(i, ho, False), 0)
        for c in hops:
            c.start()

    lax.fori_loop(0, CELLS, lambda i, _: cell_backward(i, hi, True), 0)
    step = move(tk, tr, "core")
    join(jnp.int32(1))
    join(jnp.int32(0))

    acc = gw.at[core]

    def plus(ref, *others):
        def step(s, _):
            v = ref[:, s].astype(F32)
            for o in others:
                v = v + o[:, s].astype(F32)
            ref[:, s] = v.astype(BF)
            return 0

        lax.fori_loop(0, 3, step, 0)

    def zat(d):
        return (z + 8 + d) % 8

    def xat(d):
        x = (xh * 2 + xl + 4 + d) % 4
        return x // 2, x % 2

    def a1(d):
        return acc.at[:, :, :, zat(d), 0]

    def b1(d):
        h, l = xat(d)
        return acc.at[:, h, :, :, 1, l]

    def a2(d):
        h, l = xat(d)
        return acc.at[:, h, :, z, 0, l]

    def b2(d):
        return acc.at[:, xh, :, zat(d), 1, xl]

    def plus4(ref, *others):
        def step(n, _):
            a, b = n // 2, n % 2
            v = ref[a, b].astype(F32)
            for o in others:
                v = v + o[a, b].astype(F32)
            ref[a, b] = v.astype(BF)
            return 0

        lax.fori_loop(0, 4, step, 0)

    def fold(dst, a, b):
        for s in range(3):
            dst[s] = (a[s].astype(F32) + b[s].astype(F32)).astype(BF)

    step.wait_recv()
    for a in range(2):
        for b in range(2):
            fold(tr.at[a, b], tr.at[a, b], tk.at[a, b])
    step = move(tr.at[1 - yl], ty, "y")

    za = [move(a1(4).at[:, :, :, 0], zp0.at[0], "z+"), move(a1(4).at[:, :, :, 1], zp0.at[1], "z-")]
    xa = [move(b1(2).at[0], xp0.at[0], "x+"), move(b1(2).at[1], xp0.at[1], "x-")]

    for c in za:
        c.wait_recv()
    plus4(a1(3).at[:, :, :, 0], zp0.at[0])
    plus4(a1(-3).at[:, :, :, 1], zp0.at[1])
    za = [move(a1(3), zp.at[0, 0], "z+"), move(a1(-3), zp.at[0, 1], "z-")]
    step.wait_recv()
    for b in range(2):
        fold(ty.at[b], ty.at[b], tr.at[yl, b])
    step = move(ty.at[1 - xh], tx.at[0], "xd")

    for c in xa:
        c.wait_recv()

    def plus1(ref, other):
        def step(s, _):
            ref[s] = (ref[s].astype(F32) + other[s].astype(F32)).astype(BF)
            return 0

        lax.fori_loop(0, 3, step, 0)

    plus1(b1(1).at[0], xp0.at[0])
    plus1(b1(-1).at[1], xp0.at[1])
    xa = [move(b1(1), xp.at[0], "x+"), move(b1(-1), xp.at[1], "x-")]

    step.wait_recv()
    fold(tx.at[0], tx.at[0], ty.at[xh])
    step = move(tx.at[0], tx.at[1], "xs")

    for k in (2, 1):
        for c in za:
            c.wait_recv()
        plus4(a1(k), zp.at[2 - k, 0])
        plus4(a1(-k), zp.at[2 - k, 1])
        za = [move(a1(k), zp.at[3 - k, 0], "z+"), move(a1(-k), zp.at[3 - k, 1], "z-")]

    step.wait_recv()
    fold(tz.at[0, 0], tx.at[0], tx.at[1])
    step = [move(tz.at[0, 0], tz.at[1, 0], "z+"), move(tz.at[0, 0], tz.at[1, 1], "z-")]

    for c in xa:
        c.wait_recv()
    plus(b1(0), xp.at[0], xp.at[1])
    zb = [move(b2(4).at[0], bp0.at[0], "z+"), move(b2(4).at[1], bp0.at[1], "z-")]

    for c in za:
        c.wait_recv()
    plus4(a1(0), zp.at[2, 0], zp.at[2, 1])
    xb = [move(a2(2).at[0], ap0.at[0], "x+"), move(a2(2).at[1], ap0.at[1], "x-")]

    for c in zb:
        c.wait_recv()
    plus1(b2(3).at[0], bp0.at[0])
    plus1(b2(-3).at[1], bp0.at[1])
    zb = [move(b2(3), bp.at[0, 0], "z+"), move(b2(-3), bp.at[0, 1], "z-")]

    for c in xb:
        c.wait_recv()
    plus1(a2(1).at[0], ap0.at[0])
    plus1(a2(-1).at[1], ap0.at[1])
    xb = [move(a2(1), ap.at[0], "x+"), move(a2(-1), ap.at[1], "x-")]

    for k in (2, 1):
        for c in step:
            c.wait_recv()
        step = [move(tz.at[3 - k, 0], tz.at[4 - k, 0], "z+"), move(tz.at[3 - k, 1], tz.at[4 - k, 1], "z-")]
        for c in zb:
            c.wait_recv()
        plus(b2(k), bp.at[2 - k, 0])
        plus(b2(-k), bp.at[2 - k, 1])
        zb = [move(b2(k), bp.at[3 - k, 0], "z+"), move(b2(-k), bp.at[3 - k, 1], "z-")]
    for c in xb:
        c.wait_recv()
    plus(a2(0), ap.at[0], ap.at[1])
    ya = [move(acc.at[1 - yl, xh, :, z, 0, xl], yb.at[0], "y")]
    for c in zb:
        c.wait_recv()
    plus(b2(0), bp.at[2, 0], bp.at[2, 1])
    ya.append(move(acc.at[1 - yl, xh, :, z, 1, xl], yb.at[1], "y"))
    for c in range(2):
        ya[c].wait_recv()
        for s in range(3):
            ob[core, s, z, c, xl] = (acc[yl, xh, s, z, c, xl].astype(F32) + yb[c, s].astype(F32)).astype(BF)

    for c in step:
        c.wait_recv()
    step = move(tz.at[3, 0], tz.at[4, 0], "z+")

    def both_cores(at):
        return move(at, at, "core")

    mine = ob.at[core, :, z, :, xl]
    pair = move(mine, mine, "xs")
    pair.wait_recv()
    chunk = lambda d: ob.at[core, :, zat(d)]
    last = [both_cores(chunk(0))]
    out = [move(chunk(0), chunk(0), "z+"), move(chunk(0), chunk(0), "z-")]
    for k in (1, 2):
        for c in out:
            c.wait_recv()
        out = [move(chunk(-k), chunk(-k), "z+"), move(chunk(k), chunk(k), "z-")]
        last += [both_cores(chunk(-k)), both_cores(chunk(k))]
    for c in out:
        c.wait_recv()
    out = [
        move(chunk(-3).at[:, 0], chunk(-3).at[:, 0], "z+"),
        move(chunk(3).at[:, 1], chunk(3).at[:, 1], "z-"),
    ]
    last += [both_cores(chunk(-3)), both_cores(chunk(3))]
    for c in out:
        c.wait_recv()
    last += [both_cores(chunk(4))]
    for c in last:
        c.wait_recv()
    done = pltpu.make_async_copy(ob, o_ref, local.at[0])
    done.start()
    step.wait_recv()
    for s in range(3):
        v = tz[0, 0, s].astype(F32) + tz[4, 0, s].astype(F32)
        for k in (1, 2, 3):
            v = v + tz[k, 0, s].astype(F32) + tz[k, 1, s].astype(F32)
        t_ref[s] = v
    for c in sends:
        c.wait_send()
    for c in hops:
        c.wait_send()

    def sent(cell, _):
        twin_of(cell).wait_send()
        return 0

    lax.fori_loop(0, CELLS, sent, 0)
    done.wait()


def shards(features, labels, classifier, w_mix, w_point, kernels, counts):
    _, _, y, xh, z, xl, core = place()
    image = jnp.where(y // 2 == 0, y, 3 - y) * 2 + xh
    tail = jnp.broadcast_to(counts[0].astype(BF), (3, 7, CH))
    small = jnp.concatenate([kernels, tail], axis=1)
    label = lax.dynamic_index_in_dim(labels, image, 0, keepdims=False)
    hot = jnp.broadcast_to((jnp.arange(4) == label).astype(F32)[:, None], (4, CH))
    classes = jnp.pad(jnp.stack([classifier.T, hot]), ((0, 0), (0, 4), (0, 0)))

    lead = (16, CH)
    shape = lambda *d: pltpu.VMEM(d + lead, BF)
    maps = lambda n, t=BF: pltpu.VMEM((n, ROWS, CH), t)
    n = 180
    summed, taps = pl.pallas_call(
        kernel,
        out_shape=(jax.ShapeDtypeStruct((2, 3, 8, 2, 2, 16, CH), BF), jax.ShapeDtypeStruct((3, 16, CH), F32)),
        in_specs=[pl.BlockSpec(memory_space=pl.ANY)] * 4 + [pl.BlockSpec(memory_space=pltpu.VMEM)],
        out_specs=(pl.BlockSpec(memory_space=pl.ANY), pl.BlockSpec(memory_space=pltpu.VMEM)),
        scratch_shapes=[
            pltpu.VMEM((2, CELLS, CH, CH), BF),
            pltpu.VMEM((CELLS, 16, CH), BF),
            pltpu.VMEM((GRID * GRID, CH), BF),
            maps(2),
            maps(2),
            maps(2),
            maps(CELLS),
            maps(CELLS),
            maps(CELLS),
            maps(CELLS, F32),
            pltpu.VMEM((ROWS, CH), F32),
            pltpu.VMEM((16, CH), F32),
            shape(2, 2, 2, 3, 8, 2, 2),
            shape(2, 2, 3, 8, 2, 2),
            shape(2, 2, 3),
            shape(2, 2, 3),
            shape(2, 3),
            shape(2, 3),
            shape(5, 2, 3),
            shape(2, 2, 2, 3),
            shape(3, 2, 2, 2, 3, 2),
            shape(2, 3, 8),
            shape(2, 2, 3, 8),
            shape(2, 3),
            shape(2, 2, 3),
            shape(2, 3),
            shape(3, 2, 2, 3),
            shape(2, 3),
            shape(2, 3, 8, 2, 2),
            pltpu.SemaphoreType.DMA((n,)),
            pltpu.SemaphoreType.DMA((n,)),
            pltpu.SemaphoreType.DMA((4,)),
        ],
        compiler_params=pltpu.CompilerParams(collective_id=1, has_side_effects=True, vmem_limit_bytes=62 << 20),
        name="step",
    )(features, w_mix, w_point, small, classes)
    summed = summed.reshape(2, 3, CH, CH).astype(F32)
    return summed[0], summed[1], taps[:, :9]


def solution(mesh):
    return jax.shard_map(
        shards,
        mesh=mesh,
        in_specs=(
            P("dp", None, None),
            P("dp"),
            P(),
            P("segment", None, None),
            P("segment", None, None),
            P("segment", None, None),
            P("segment"),
        ),
        out_specs=(P("segment", None, None), P("segment", None, None), P("segment", None, None)),
        check_vma=False,
    )
```

```python
import jax
import jax.numpy as jnp
from jax import lax
from jax.experimental import pallas as pl
from jax.experimental.pallas import tpu as pltpu
from jax.sharding import PartitionSpec as P

GRID = 12
PITCH = 16
ROWS = GRID * PITCH
CH = 512
CELLS = 12
EPSILON = 1e-06
MESH = pl.DeviceIdType.MESH
BF = jnp.bfloat16
F32 = jnp.float32


def place():
    seg, dp = lax.axis_index("segment"), lax.axis_index("dp")
    y, xh = seg // 2, seg % 2
    core, xl, z = dp % 2, (dp // 2) % 2, dp // 4
    return seg, dp, y, xh, z, xl, core


def dev(y, xh, z, xl, core):
    return (y * 2 + xh, (z * 2 + xl) * 2 + core)


def neighbours():
    seg, dp, y, xh, z, xl, core = place()
    yp = y + 1 - 2 * (y % 2)
    return {
        "core": dev(y, xh, z, xl, 1 - core),
        "xs": dev(y, xh, z, 1 - xl, core),
        "xd": dev(y, 1 - xh, z, 1 - xl, core),
        "x+": dev(y, jnp.where(xl == 0, xh, 1 - xh), z, 1 - xl, core),
        "x-": dev(y, jnp.where(xl == 1, xh, 1 - xh), z, 1 - xl, core),
        "z+": dev(y, xh, (z + 1) % 8, xl, core),
        "z-": dev(y, xh, (z + 7) % 8, xl, core),
        "y": dev(yp, xh, z, xl, core),
        "hop": dev(3 - y, xh, z, xl, core),
    }


def greet(names, near):
    barrier = pltpu.get_barrier_semaphore()
    for name in names:
        pl.semaphore_signal(barrier, inc=1, device_id=near[name], device_id_type=MESH)
    pl.semaphore_wait(barrier, len(names))


def remote(src, dst, send, recv, i, target):
    return pltpu.make_async_remote_copy(
        src_ref=src, dst_ref=dst, send_sem=send.at[i], recv_sem=recv.at[i], device_id=target, device_id_type=MESH
    )


def down(r):
    return jnp.concatenate([jnp.zeros((PITCH, r.shape[1]), r.dtype), r[:-PITCH]], axis=0)


def up(r):
    return jnp.concatenate([r[PITCH:], jnp.zeros((PITCH, r.shape[1]), r.dtype)], axis=0)


NT = (((1,), (1,)), ((), ()))
TN = (((0,), (0,)), ((), ()))


def parts_of(cell):
    return cell // 6, (cell // 3) % 2, cell % 3


def kernel(
    f_ref, mix_ref, point_ref, small_ref, class_ref, label_ref, o_ref, t_ref,
    w_ref, s_ref, img, st, gb, ho, hi, sp, so, ss, tt, gs, taps, gw, rb,
    tk, tr, ty, tx, tz, zp0, zp, xp0, xp, ap0, ap, bp0, bp, yb, ob, send, recv, local,
):
    _, _, y, xh, z, xl, core = place()
    near = neighbours()
    stage, yl, zpar = y // 2, y % 2, z % 2
    image = jnp.where(stage == 0, y, 3 - y) * 2 + xh
    own = yl * 2 + xh
    sec_y, sec_x, sec_xy = (1 - yl) * 2 + xh, yl * 2 + (1 - xh), (1 - yl) * 2 + (1 - xh)
    count = [14]
    sends = []

    def move(src, dst, name):
        c = remote(src, dst, send, recv, count[0], near[name])
        count[0] += 1
        sends.append(c)
        c.start()
        return c

    def spread(pixels, dst, i):
        for r in range(GRID):
            row = jnp.concatenate([pixels[GRID * r : GRID * r + GRID], jnp.zeros((PITCH - GRID, CH), F32)], axis=0)
            dst[i, PITCH * r : PITCH * r + PITCH] = row.astype(BF)

    def packed(maps, i):
        pixels = maps[i].astype(F32)
        return jnp.concatenate([pixels[PITCH * r : PITCH * r + GRID] for r in range(GRID)], axis=0).astype(BF)

    loc = [
        pltpu.make_async_copy(small_ref, s_ref.at[pl.ds(own * 3, 3)], local.at[2]),
        pltpu.make_async_copy(mix_ref, w_ref.at[0, pl.ds(own * 3, 3)], local.at[0]),
        pltpu.make_async_copy(point_ref, w_ref.at[1, pl.ds(own * 3, 3)], local.at[1]),
        pltpu.make_async_copy(f_ref.at[image], img, local.at[3]),
    ]
    for c in loc:
        c.start()
    greet(("core", "xs", "xd", "z+", "z-", "y", "hop"), near)
    for c in loc:
        c.wait()

    def go(sec, slot, row, count, name):
        at = w_ref.at[core, sec * 3 + slot, pl.ds(pl.multiple_of(row, 16), count)]
        return move(at, at, name)

    def tiny(sec, name):
        at = s_ref.at[pl.ds(sec * 3, 3)]
        return move(at, at, name)

    mine, other = 128 * (2 * zpar + xl), 128 * (2 * zpar + 1 - xl)

    def to_z(sec, slot, row):
        return [go(sec, slot, row, 64, "z+"), go(sec, slot, row + 64, 64, "z-")]

    t_y, t_x = tiny(own, "y"), tiny(own, "xd")
    x1, y_first, y_then, x2, xy1, xy2, zx, zy, zxy, twin = [], [], [], [], [], [], [], [], [], []
    for s in range(3):
        x1.append(go(own, s, other, 128, "xd"))
        y_first.append(go(own, s, other, 128, "y"))
    for s in range(3):
        y_then.append(go(own, s, mine, 128, "y"))
    t_y.wait_recv()
    t_xy = tiny(sec_y, "xd")
    for s in range(3):
        x1[s].wait_recv()
        x2.append(go(sec_x, s, mine, 128, "xs"))
        zx.append(to_z(sec_x, s, mine))
        y_first[s].wait_recv()
        xy1.append(go(sec_y, s, other, 128, "xd"))
        zy.append(to_z(sec_y, s, other))
    for s in range(3):
        x2[s].wait_recv()
        zx[s] += to_z(sec_x, s, other)
        twin.append(go(sec_x, s, 256 * zpar, 256, "core"))
    for s in range(3):
        xy1[s].wait_recv()
        xy2.append(go(sec_xy, s, mine, 128, "xs"))
        zxy.append(to_z(sec_xy, s, mine))
        y_then[s].wait_recv()
        zy[s] += to_z(sec_y, s, mine)
        twin.append(go(sec_y, s, 256 * zpar, 256, "core"))
    for s in range(3):
        xy2[s].wait_recv()
        zxy[s] += to_z(sec_xy, s, other)
        twin.append(go(sec_xy, s, 256 * zpar, 256, "core"))
    for sec, group in ((sec_x, zx), (sec_y, zy), (sec_xy, zxy)):
        for s in range(3):
            for c in group[s]:
                c.wait_recv()
            twin.append(go(sec, s, 256 * (1 - zpar), 256, "core"))

    image_in = img[...].astype(F32)
    spread(image_in, st, 0)
    spread(image_in, st, 1)
    for c in twin + [t_x, t_xy]:
        c.wait_recv()

    hops = [remote(ho.at[i], hi.at[i], send, recv, 12 + i, near["hop"]) for i in range(2)]
    real = lax.broadcasted_iota(jnp.int32, (ROWS, 128), 0) % PITCH < GRID

    def holds(cell, cols=slice(None)):
        return s_ref[cell, 9:10, cols].astype(F32) > (cell % 3).astype(F32)

    def cell_forward(cell, _):
        sp[cell] = st[0]
        so[cell] = st[1]
        for c in range(4):
            cols = slice(128 * c, 128 * c + 128)
            a = jnp.maximum(st[1, :, cols].astype(F32), 0.0)
            k = s_ref[cell, :, cols].astype(F32)
            am, ap_ = pltpu.roll(a, 1, 0), pltpu.roll(a, ROWS - 1, 0)
            r = [k[3 * u : 3 * u + 1] * am + k[3 * u + 1 : 3 * u + 2] * a + k[3 * u + 2 : 3 * u + 3] * ap_ for u in range(3)]
            s = r[1] + down(r[0]) + up(r[2])
            ss[cell, :, cols] = jnp.where(real, s, 0.0).astype(BF)
        prev = st[0]
        total = jnp.dot(ss[cell], w_ref[1, cell], preferred_element_type=F32)
        total = total + jnp.dot(jnp.maximum(prev, 0), w_ref[0, cell], preferred_element_type=F32)
        prev = prev.astype(F32)
        total = prev + total
        q = lax.rsqrt(jnp.mean(total * total, axis=-1, keepdims=True) + EPSILON)
        tt[cell] = total
        on = holds(cell)
        st[1] = jnp.where(on, prev, st[1].astype(F32)).astype(BF)
        st[0] = jnp.where(on, total * q, prev).astype(BF)
        return 0

    def head():
        last = st[0].astype(F32)
        pooled = jnp.sum(jnp.maximum(last, 0.0), axis=0, keepdims=True) / (GRID * GRID)
        pooled = jnp.broadcast_to(pooled, (8, CH))
        classes = class_ref[...]
        logits = lax.dot_general(pooled, classes, NT, precision=lax.Precision.HIGHEST, preferred_element_type=F32)
        label = label_ref[image].astype(F32)
        away = jnp.abs(lax.broadcasted_iota(jnp.int32, logits.shape, 1).astype(F32) - label)
        miss = logits - jnp.maximum(1.0 - away, 0.0)
        grad = jnp.dot(miss, classes, precision=lax.Precision.HIGHEST, preferred_element_type=F32)
        grad = grad[:1] / (GRID * GRID)
        st[0] = jnp.where(last > 0, jnp.broadcast_to(grad, last.shape), 0.0).astype(BF)
        st[1] = jnp.zeros((ROWS, CH), BF)

    def twin_of(cell):
        a, b, s = parts_of(cell)
        return remote(gw.at[1 - core, a, b, s], rb.at[a, b, s], send, recv, cell, near["core"])

    def join(cell):
        a, b, s = parts_of(cell)
        twin_of(cell).wait_recv()
        gw[core, a, b, s] = (gw[core, a, b, s].astype(F32) + rb[a, b, s].astype(F32)).astype(BF)

    def cell_backward(i, g, wgrad):
        cell = CELLS - 1 - i
        a_, b_, s_ = parts_of(cell)
        total = tt[cell]
        q = lax.rsqrt(jnp.mean(total * total, axis=-1, keepdims=True) + EPSILON)
        n = total * q
        gn = g[0].astype(F32)
        on = holds(cell)
        gt = q * (gn - n * jnp.mean(gn * n, axis=-1, keepdims=True))
        gt = jnp.where(on, gt, 0.0)
        gh = gt.astype(BF)
        gs[...] = lax.dot_general(gh, w_ref[1, cell], NT, preferred_element_type=F32)
        gm = lax.dot_general(gh, w_ref[0, cell], NT, preferred_element_type=F32)
        prev = sp[cell]
        g[0] = jnp.where(on, gt + jnp.where(prev > 0, gm, 0.0) + g[1].astype(F32), gn).astype(BF)
        for c in range(4):
            cols = slice(128 * c, 128 * c + 128)
            u_ = gs[:, cols]
            k = s_ref[cell, :, cols].astype(F32)
            gv = [pltpu.roll(u_, ROWS - 1, 0), u_, pltpu.roll(u_, 1, 0)]
            r = [
                k[3 * u : 3 * u + 1] * gv[0] + k[3 * u + 1 : 3 * u + 2] * gv[1] + k[3 * u + 2 : 3 * u + 3] * gv[2]
                for u in range(3)
            ]
            rel = r[1] + up(r[0]) + down(r[2])
            older = so[cell, :, cols].astype(F32)
            g[1, :, cols] = jnp.where(holds(cell, cols), jnp.where(older > 0, rel, 0.0), g[1, :, cols].astype(F32)).astype(BF)
            if wgrad:
                a = jnp.maximum(older, 0.0)
                for v in range(3):
                    taps[v : v + 1, cols] = jnp.sum(a[:-PITCH] * gv[v][PITCH:], axis=0, keepdims=True)
                    taps[3 + v : 4 + v, cols] = jnp.sum(a * gv[v], axis=0, keepdims=True)
                    taps[6 + v : 7 + v, cols] = jnp.sum(a[PITCH:] * gv[v][:-PITCH], axis=0, keepdims=True)
        if wgrad:
            tk[a_, b_, s_] = taps[...].astype(BF)
            parts = (8, 2, 2, 16, CH)
            gw[0, a_, b_, s_] = (
                lax.dot_general(jnp.maximum(prev, 0), gh, TN, preferred_element_type=F32).astype(BF).reshape(parts)
            )
            gw[1, a_, b_, s_] = lax.dot_general(ss[cell], gh, TN, preferred_element_type=F32).astype(BF).reshape(parts)
            twin_of(cell).start()

            @pl.when(i >= 1)
            def _():
                join(cell + 1)

            for at, steps in during.items():

                @pl.when(i == at)
                def _(steps=steps):
                    for way, group, s, k in steps:
                        way(group, s, k)

        return 0

    acc = gw.at[core]
    table = {}

    def define(key, make):
        table[key] = (make, count[0])
        count[0] += 1

    def copy(key):
        make, index = table[key]
        source, target, name = make()
        return remote(source, target, send, recv, index, near[name])

    def start(*keys):
        for key in keys:
            copy(key).start()

    def wait(*keys):
        for key in keys:
            copy(key).wait_recv()

    def zat(d):
        return (z + 8 + d) % 8

    def xat(d):
        x = (xh * 2 + xl + 4 + d) % 4
        return x // 2, x % 2

    def a1(g, s, d):
        return acc.at[g, :, s, zat(d), 0]

    def b1(g, s, d):
        h, l = xat(d)
        return acc.at[g, h, s, :, 1, l]

    def a2(g, d):
        h, l = xat(d)
        return acc.at[g, h, :, z, 0, l]

    def b2(g, d):
        return acc.at[g, xh, :, zat(d), 1, xl]

    def plus(ref, *others):
        v = ref[...].astype(F32)
        for o in others:
            v = v + o[...].astype(F32)
        ref[...] = v.astype(BF)

    SIGN = (1, -1)
    ZDIR, XDIR = ("z+", "z-"), ("x+", "x-")
    PART = (pl.ds(0, 2), pl.ds(2, 1))
    for g in (1, 0):
        for w in range(2):
            half = pl.ds(4 * w, 4)
            for s in range(3):
                define(("za", g, s, 0, w), lambda g=g, s=s, w=w: (a1(g, s, 4).at[:, w], zp0.at[g, w, s], ZDIR[w]))
                for k in (1, 2, 3):
                    define(
                        ("za", g, s, k, w),
                        lambda g=g, s=s, w=w, k=k: (a1(g, s, SIGN[w] * (4 - k)), zp.at[g, k - 1, w, s], ZDIR[w]),
                    )
                define(
                    ("xb", g, s, 0, w), lambda g=g, s=s, w=w, half=half: (b1(g, s, 2).at[half], xp0.at[g, w, s], XDIR[w])
                )
                define(("xb", g, s, 1, w), lambda g=g, s=s, w=w: (b1(g, s, SIGN[w]), xp.at[g, w, s], XDIR[w]))
            define(("xa", g, 0, w), lambda g=g, w=w: (a2(g, 2).at[PART[w]], ap0.at[g, PART[w]], XDIR[w]))
            define(("xa", g, 1, w), lambda g=g, w=w: (a2(g, SIGN[w]), ap.at[g, w], XDIR[w]))
            define(("zb", g, 0, w), lambda g=g, w=w: (b2(g, 4).at[PART[w]], bp0.at[g, PART[w]], ZDIR[w]))
            for k in (1, 2, 3):
                define(("zb", g, k, w), lambda g=g, w=w, k=k: (b2(g, SIGN[w] * (4 - k)), bp.at[g, k - 1, w], ZDIR[w]))
    for c in range(2):
        define(("y", c), lambda c=c: (acc.at[1 - yl, xh, :, z, c, xl], yb.at[c], "y"))

    def both(*key):
        return (*key, 0), (*key, 1)

    def ring_z(g, s, k):
        if k == 1:
            start(*both("za", g, s, 0))
        else:
            wait(*both("za", g, s, k - 2))
            for w in range(2):
                if k == 2:
                    plus(a1(g, s, SIGN[w] * 3).at[:, w], zp0.at[g, w, s])
                else:
                    plus(a1(g, s, SIGN[w] * (5 - k)), zp.at[g, k - 3, w, s])
            start(*both("za", g, s, k - 1))

    def ring_x(g, s, k):
        if k == 1:
            start(*both("xb", g, s, 0))
        else:
            wait(*both("xb", g, s, 0))
            for w in range(2):
                plus(b1(g, s, SIGN[w]).at[pl.ds(4 * w, 4)], xp0.at[g, w, s])
            start(*both("xb", g, s, 1))

    def along_z(g, k):
        if k == 5:
            for s in range(3):
                wait(*both("za", g, s, 3))
                plus(a1(g, s, 0), zp.at[g, 2, 0, s], zp.at[g, 2, 1, s])
            start(*both("xa", g, 0))
        elif k == 6:
            wait(*both("xa", g, 0))
            for w in range(2):
                plus(a2(g, SIGN[w]).at[PART[w]], ap0.at[g, PART[w]])
            start(*both("xa", g, 1))
        else:
            wait(*both("xa", g, 1))
            plus(a2(g, 0), ap.at[g, 0], ap.at[g, 1])

            @pl.when(yl != g)
            def _():
                start(("y", 0))

    def along_x(g, k):
        if k == 3:
            for s in range(3):
                wait(*both("xb", g, s, 1))
                plus(b1(g, s, 0), xp.at[g, 0, s], xp.at[g, 1, s])
            start(*both("zb", g, 0))
        elif k <= 6:
            wait(*both("zb", g, k - 4))
            for w in range(2):
                if k == 4:
                    plus(b2(g, SIGN[w] * 3).at[PART[w]], bp0.at[g, PART[w]])
                else:
                    plus(b2(g, SIGN[w] * (7 - k)), bp.at[g, k - 5, w])
            start(*both("zb", g, k - 3))
        else:
            wait(*both("zb", g, 3))
            plus(b2(g, 0), bp.at[g, 2, 0], bp.at[g, 2, 1])

            @pl.when(yl != g)
            def _():
                start(("y", 1))

    z_, x_ = ring_z, ring_x
    during = {
        4: [(z_, 1, 2, 1), (x_, 1, 2, 1)],
        5: [(z_, 1, 1, 1), (x_, 1, 1, 1)],
        6: [(z_, 1, 0, 1), (x_, 1, 0, 1), (z_, 1, 2, 2)],
        7: [(z_, 1, 1, 2), (x_, 1, 2, 2)],
        8: [(z_, 1, 0, 2), (z_, 1, 2, 3), (x_, 1, 1, 2)],
        9: [(z_, 1, 1, 3), (x_, 1, 0, 2)],
        10: [(z_, 0, 2, 1), (x_, 0, 2, 1), (z_, 1, 0, 3), (z_, 1, 2, 4)],
        11: [(z_, 0, 1, 1), (x_, 0, 1, 1), (z_, 1, 1, 4)],
    }

    taps[...] = jnp.zeros_like(taps)

    @pl.when(stage == 1)
    def _():
        for c in hops:
            c.wait_recv()
        for i in range(2):
            spread(hi[i].astype(F32), st, i)

    lax.fori_loop(0, CELLS, cell_forward, 0)

    @pl.when(stage == 0)
    def _():
        for i in range(2):
            ho[i] = packed(st, i)
            hops[i].start()
        for i in range(2):
            hops[i].wait_recv()
            spread(hi[i].astype(F32), gb, i)

    @pl.when(stage == 1)
    def _():
        head()
        gb[...] = st[...]
        lax.fori_loop(0, CELLS, lambda i, _: cell_backward(i, st, False), 0)
        for i in range(2):
            ho[i] = packed(st, i)
            hops[i].start()

    lax.fori_loop(0, CELLS, lambda i, _: cell_backward(i, gb, True), 0)
    join(jnp.int32(0))
    z_(0, 0, 1)
    x_(0, 0, 1)
    step = move(tk, tr, "core")

    def fold(dst, a, b):
        for s in range(3):
            dst[s] = (a[s].astype(F32) + b[s].astype(F32)).astype(BF)

    z_(1, 0, 4)
    z_(0, 2, 2)
    x_(0, 2, 2)
    along_x(1, 3)
    step.wait_recv()
    for a in range(2):
        for b in range(2):
            fold(tr.at[a, b], tr.at[a, b], tk.at[a, b])
    step = move(tr.at[1 - yl], ty, "y")
    z_(0, 1, 2)
    x_(0, 1, 2)
    along_z(1, 5)
    z_(0, 0, 2)
    x_(0, 0, 2)
    along_x(1, 4)
    step.wait_recv()
    for b in range(2):
        fold(ty.at[b], ty.at[b], tr.at[yl, b])
    step = move(ty.at[1 - xh], tx.at[0], "xd")
    z_(0, 2, 3)
    along_z(1, 6)
    z_(0, 1, 3)
    along_x(1, 5)
    z_(0, 0, 3)
    step.wait_recv()
    fold(tx.at[0], tx.at[0], ty.at[xh])
    step = move(tx.at[0], tx.at[1], "xs")
    along_x(0, 3)
    along_z(1, 7)
    z_(0, 2, 4)
    along_x(1, 6)
    z_(0, 1, 4)
    along_x(0, 4)
    z_(0, 0, 4)
    along_x(1, 7)
    step.wait_recv()
    fold(tz.at[0, 0], tx.at[0], tx.at[1])
    step = [move(tz.at[0, 0], tz.at[1, 0], "z+"), move(tz.at[0, 0], tz.at[1, 1], "z-")]
    along_x(0, 5)
    along_z(0, 5)
    for c in step:
        c.wait_recv()
    step = [move(tz.at[1, 0], tz.at[2, 0], "z+"), move(tz.at[1, 1], tz.at[2, 1], "z-")]
    along_x(0, 6)
    along_z(0, 6)
    along_z(0, 7)

    def landed(c):
        wait(("y", c))
        for s in range(3):
            ob[core, s, z, c, xl] = (acc[yl, xh, s, z, c, xl].astype(F32) + yb[c, s].astype(F32)).astype(BF)

    last = []

    def to(at, name):
        return move(at, at, name)

    def to_twin(at):
        last.append(to(at, "core"))

    def chunk(d):
        return ob.at[core, :, zat(d), 0]

    def piece(d):
        return ob.at[core, :, zat(d), 1, xl]

    def arrived(copies):
        for c in copies:
            c.wait_recv()

    landed(0)
    pair = to(ob.at[core, :, z, 0, xl], "xs")
    along_x(0, 7)
    arrived(step)
    step = [move(tz.at[2, 0], tz.at[3, 0], "z+"), move(tz.at[2, 1], tz.at[3, 1], "z-")]
    arrived([pair])
    out0 = [to(chunk(0), "z+"), to(chunk(0), "z-")]
    to_twin(chunk(0))
    landed(1)
    out1 = [to(piece(0), "z+"), to(piece(0), "z-")]
    side = [(0, to(piece(0), "xs"))]
    for k in (1, 2):
        arrived(out0)
        out0 = [to(chunk(-k), "z+"), to(chunk(k), "z-")]
        to_twin(chunk(-k))
        to_twin(chunk(k))
        arrived(out1)
        out1 = [to(piece(-k), "z+"), to(piece(k), "z-")]
        side += [(-k, to(piece(-k), "xs")), (k, to(piece(k), "xs"))]
    arrived(out0)
    out0 = [to(chunk(-3).at[:, 0], "z+"), to(chunk(3).at[:, 1], "z-")]
    to_twin(chunk(-3))
    to_twin(chunk(3))
    arrived(out1)
    out1 = [to(piece(-3).at[PART[0]], "z+"), to(piece(3).at[PART[1]], "z-")]
    side += [(-3, to(piece(-3), "xs")), (3, to(piece(3), "xs"))]
    arrived(step)
    step = move(tz.at[3, 0], tz.at[4, 0], "z+")
    arrived(out0)
    to_twin(chunk(4))
    arrived(out1)
    side += [(4, to(piece(4), "xs"))]
    for d, c in side:
        c.wait_recv()
        to_twin(ob.at[core, :, zat(d), 1])
    step.wait_recv()
    for s in range(3):
        v = tz[0, 0, s].astype(F32) + tz[4, 0, s].astype(F32)
        for k in (1, 2, 3):
            v = v + tz[k, 0, s].astype(F32) + tz[k, 1, s].astype(F32)
        t_ref[s] = v
    arrived(last)
    done = pltpu.make_async_copy(ob, o_ref, local.at[0])
    done.start()
    done.wait()
    for c in sends:
        c.wait_send()
    for c in hops:
        c.wait_send()
    for key in table:
        copy(key).wait_send()

    def sent(cell, _):
        twin_of(cell).wait_send()
        return 0

    lax.fori_loop(0, CELLS, sent, 0)


def shards(features, labels, classifier, w_mix, w_point, kernels, counts):
    tail = jnp.broadcast_to(counts[0].astype(BF), (3, 7, CH))
    small = jnp.concatenate([kernels, tail], axis=1)

    lead = (16, CH)
    shape = lambda *d: pltpu.VMEM(d + lead, BF)
    maps = lambda n, t=BF: pltpu.VMEM((n, ROWS, CH), t)
    n = 256
    summed, taps = pl.pallas_call(
        kernel,
        out_shape=(jax.ShapeDtypeStruct((2, 3, 8, 2, 2, 16, CH), BF), jax.ShapeDtypeStruct((3, 16, CH), F32)),
        in_specs=[pl.BlockSpec(memory_space=pl.ANY)] * 4
        + [pl.BlockSpec(memory_space=pltpu.VMEM), pl.BlockSpec(memory_space=pltpu.SMEM)],
        out_specs=(pl.BlockSpec(memory_space=pl.ANY), pl.BlockSpec(memory_space=pltpu.VMEM)),
        scratch_shapes=[
            pltpu.VMEM((2, CELLS, CH, CH), BF),
            pltpu.VMEM((CELLS, 16, CH), BF),
            pltpu.VMEM((GRID * GRID, CH), BF),
            maps(2),
            maps(2),
            pltpu.VMEM((2, GRID * GRID, CH), BF),
            pltpu.VMEM((2, GRID * GRID, CH), BF),
            maps(CELLS),
            maps(CELLS),
            maps(CELLS),
            maps(CELLS, F32),
            pltpu.VMEM((ROWS, CH), F32),
            pltpu.VMEM((16, CH), F32),
            shape(2, 2, 2, 3, 8, 2, 2),
            shape(2, 2, 3, 8, 2, 2),
            shape(2, 2, 3),
            shape(2, 2, 3),
            shape(2, 3),
            shape(2, 3),
            shape(5, 2, 3),
            shape(2, 2, 3, 2),
            shape(2, 3, 2, 3, 2, 2),
            shape(2, 2, 3, 4),
            shape(2, 2, 3, 8),
            shape(2, 3),
            shape(2, 2, 3),
            shape(2, 3),
            shape(2, 3, 2, 3),
            shape(2, 3),
            shape(2, 3, 8, 2, 2),
            pltpu.SemaphoreType.DMA((n,)),
            pltpu.SemaphoreType.DMA((n,)),
            pltpu.SemaphoreType.DMA((4,)),
        ],
        compiler_params=pltpu.CompilerParams(collective_id=1, has_side_effects=True, vmem_limit_bytes=62 << 20),
        name="step",
    )(features, w_mix, w_point, small, classifier.T, labels)
    summed = summed.reshape(2, 3, CH, CH).astype(F32)
    return summed[0], summed[1], taps[:, :9]


def solution(mesh):
    return jax.shard_map(
        shards,
        mesh=mesh,
        in_specs=(
            P("dp", None, None),
            P("dp"),
            P(),
            P("segment", None, None),
            P("segment", None, None),
            P("segment", None, None),
            P("segment"),
        ),
        out_specs=(P("segment", None, None), P("segment", None, None), P("segment", None, None)),
        check_vma=False,
    )
```

```python
import jax
import jax.numpy as jnp
from jax import lax
from jax.experimental import pallas as pl
from jax.experimental.pallas import tpu as pltpu
from jax.sharding import PartitionSpec as P

GRID = 12
PITCH = 16
ROWS = GRID * PITCH
CH = 512
CELLS = 12
EPSILON = 1e-06
MESH = pl.DeviceIdType.MESH
VMEM_MB = 62
SEMAPHORES = 300
Z_LATE = (1, 3, 5, 7)
X_LATE = 7
BF = jnp.bfloat16
F32 = jnp.float32


def place():
    seg, dp = lax.axis_index("segment"), lax.axis_index("dp")
    y, xh = seg // 2, seg % 2
    core, xl, z = dp % 2, (dp // 2) % 2, dp // 4
    return seg, dp, y, xh, z, xl, core


def dev(y, xh, z, xl, core):
    return (y * 2 + xh, (z * 2 + xl) * 2 + core)


def neighbours():
    seg, dp, y, xh, z, xl, core = place()
    yp = y + 1 - 2 * (y % 2)
    return {
        "core": dev(y, xh, z, xl, 1 - core),
        "xs": dev(y, xh, z, 1 - xl, core),
        "xd": dev(y, 1 - xh, z, 1 - xl, core),
        "x+": dev(y, jnp.where(xl == 0, xh, 1 - xh), z, 1 - xl, core),
        "x-": dev(y, jnp.where(xl == 1, xh, 1 - xh), z, 1 - xl, core),
        "z+": dev(y, xh, (z + 1) % 8, xl, core),
        "z-": dev(y, xh, (z + 7) % 8, xl, core),
        "z4": dev(y, xh, (z + 4) % 8, xl, core),
        "x2": dev(y, 1 - xh, z, xl, core),
        "y": dev(yp, xh, z, xl, core),
        "hop": dev(3 - y, xh, z, xl, core),
    }


def greet(names, near):
    barrier = pltpu.get_barrier_semaphore()
    for name in names:
        pl.semaphore_signal(barrier, inc=1, device_id=near[name], device_id_type=MESH)
    pl.semaphore_wait(barrier, len(names))


def remote(src, dst, send, recv, i, target):
    return pltpu.make_async_remote_copy(
        src_ref=src, dst_ref=dst, send_sem=send.at[i], recv_sem=recv.at[i], device_id=target, device_id_type=MESH
    )


def down(r):
    return jnp.concatenate([jnp.zeros((PITCH, r.shape[1]), r.dtype), r[:-PITCH]], axis=0)


def up(r):
    return jnp.concatenate([r[PITCH:], jnp.zeros((PITCH, r.shape[1]), r.dtype)], axis=0)


NT = (((1,), (1,)), ((), ()))
TN = (((0,), (0,)), ((), ()))


def parts_of(cell):
    return cell // 6, (cell // 3) % 2, cell % 3


def kernel(
    f_ref, mix_ref, point_ref, tap_ref, class_ref, label_ref, count_ref, o_ref, t_ref,
    w_ref, s_ref, img, tin, st, gb, ho, hi, sp, so, ss, tt, gs, taps, gw, rb,
    tk, tr, ty, tx, tz, zp0, zp, xp0, xp, ap0, ap, bp0, bp, yb, ob, send, recv, local,
):
    _, _, y, xh, z, xl, core = place()
    near = neighbours()
    stage, yl, zpar = y // 2, y % 2, z % 2
    image = jnp.where(stage == 0, y, 3 - y) * 2 + xh
    own = yl * 2 + xh
    sec_y, sec_x, sec_xy = (1 - yl) * 2 + xh, yl * 2 + (1 - xh), (1 - yl) * 2 + (1 - xh)
    count = [14]
    sends = []

    def move(src, dst, name):
        c = remote(src, dst, send, recv, count[0], near[name])
        count[0] += 1
        sends.append(c)
        c.start()
        return c

    def spread(pixels, dst, i):
        for r in range(GRID):
            row = jnp.concatenate([pixels[GRID * r : GRID * r + GRID], jnp.zeros((PITCH - GRID, CH), F32)], axis=0)
            dst[i, PITCH * r : PITCH * r + PITCH] = row.astype(BF)

    def packed(maps, i):
        pixels = maps[i].astype(F32)
        return jnp.concatenate([pixels[PITCH * r : PITCH * r + GRID] for r in range(GRID)], axis=0).astype(BF)

    loc = [
        pltpu.make_async_copy(tap_ref, tin, local.at[2]),
        pltpu.make_async_copy(mix_ref, w_ref.at[0, pl.ds(own * 3, 3)], local.at[0]),
        pltpu.make_async_copy(point_ref, w_ref.at[1, pl.ds(own * 3, 3)], local.at[1]),
        pltpu.make_async_copy(f_ref.at[image], img, local.at[3]),
    ]
    for c in loc:
        c.start()
    greet(("core", "xs", "xd", "z+", "z-", "z4", "x2", "y", "hop"), near)
    for c in loc:
        c.wait()
    many = jnp.full((7, CH), count_ref[0].astype(F32), F32)
    for s in range(3):
        s_ref[own * 3 + s] = jnp.concatenate([tin[s].astype(F32), many], axis=0).astype(BF)

    def go(sec, slot, row, count, name):
        at = w_ref.at[core, sec * 3 + slot, pl.ds(pl.multiple_of(row, 16), count)]
        return move(at, at, name)

    def tiny(sec, name):
        at = s_ref.at[pl.ds(sec * 3, 3)]
        return move(at, at, name)

    mine, other = 128 * (2 * zpar + xl), 128 * (2 * zpar + 1 - xl)

    def to_z(sec, slot, row):
        return [go(sec, slot, row, 64, "z+"), go(sec, slot, row + 64, 64, "z-")]

    t_y, t_x = tiny(own, "y"), tiny(own, "xd")
    x1, y_first, y_then, x2, xy1, xy2, zx, zy, zxy, twin = [], [], [], [], [], [], [], [], [], []
    for s in range(3):
        x1.append(go(own, s, other, 128, "xd"))
        y_first.append(go(own, s, other, 128, "y"))
    for s in range(3):
        y_then.append(go(own, s, mine, 128, "y"))
    y_rest = go(own, 2, 256 * (1 - zpar), 256, "y")
    t_y.wait_recv()
    t_xy = tiny(sec_y, "xd")
    for s in range(3):
        x1[s].wait_recv()
        x2.append(go(sec_x, s, mine, 128, "xs"))
        zx.append(to_z(sec_x, s, mine))
        y_first[s].wait_recv()
        xy1.append(go(sec_y, s, other, 128, "xd"))
        zy.append(to_z(sec_y, s, other) if s < 2 else [y_rest])
    for s in range(3):
        x2[s].wait_recv()
        zx[s] += to_z(sec_x, s, other)
        twin.append(go(sec_x, s, 256 * zpar, 256, "core"))
    for s in range(3):
        xy1[s].wait_recv()
        xy2.append(go(sec_xy, s, mine, 128, "xs"))
        zxy.append(to_z(sec_xy, s, mine))
        y_then[s].wait_recv()
        if s < 2:
            zy[s] += to_z(sec_y, s, mine)
        twin.append(go(sec_y, s, 256 * zpar, 256, "core"))
    for s in range(3):
        xy2[s].wait_recv()
        zxy[s] += to_z(sec_xy, s, other)
        twin.append(go(sec_xy, s, 256 * zpar, 256, "core"))
    for sec, group in ((sec_x, zx), (sec_y, zy), (sec_xy, zxy)):
        for s in range(3):
            for c in group[s]:
                c.wait_recv()
            twin.append(go(sec, s, 256 * (1 - zpar), 256, "core"))

    image_in = img[...].astype(F32)
    spread(image_in, st, 0)
    spread(image_in, st, 1)
    for c in twin + [t_x, t_xy]:
        c.wait_recv()

    hops = [remote(ho.at[i], hi.at[i], send, recv, 12 + i, near["hop"]) for i in range(2)]
    real = lax.broadcasted_iota(jnp.int32, (ROWS, 128), 0) % PITCH < GRID

    def holds(cell, cols=slice(None)):
        return s_ref[cell, 9:10, cols].astype(F32) > (cell % 3).astype(F32)

    def cell_forward(cell, _):
        sp[cell] = st[0]
        so[cell] = st[1]
        for c in range(4):
            cols = slice(128 * c, 128 * c + 128)
            a = jnp.maximum(st[1, :, cols].astype(F32), 0.0)
            k = s_ref[cell, :, cols].astype(F32)
            am, ap_ = pltpu.roll(a, 1, 0), pltpu.roll(a, ROWS - 1, 0)
            r = [k[3 * u : 3 * u + 1] * am + k[3 * u + 1 : 3 * u + 2] * a + k[3 * u + 2 : 3 * u + 3] * ap_ for u in range(3)]
            s = r[1] + down(r[0]) + up(r[2])
            ss[cell, :, cols] = jnp.where(real, s, 0.0).astype(BF)
        prev = st[0]
        total = jnp.dot(ss[cell], w_ref[1, cell], preferred_element_type=F32)
        total = total + jnp.dot(jnp.maximum(prev, 0), w_ref[0, cell], preferred_element_type=F32)
        prev = prev.astype(F32)
        total = prev + total
        q = lax.rsqrt(jnp.mean(total * total, axis=-1, keepdims=True) + EPSILON)
        tt[cell] = total
        on = holds(cell)
        st[1] = jnp.where(on, prev, st[1].astype(F32)).astype(BF)
        st[0] = jnp.where(on, total * q, prev).astype(BF)
        return 0

    def head():
        last = st[0].astype(F32)
        pooled = jnp.sum(jnp.maximum(last, 0.0), axis=0, keepdims=True) / (GRID * GRID)
        pooled = jnp.broadcast_to(pooled, (8, CH))
        classes = class_ref[...]
        logits = lax.dot_general(pooled, classes, NT, precision=lax.Precision.HIGHEST, preferred_element_type=F32)
        label = label_ref[image].astype(F32)
        away = jnp.abs(lax.broadcasted_iota(jnp.int32, logits.shape, 1).astype(F32) - label)
        miss = logits - jnp.maximum(1.0 - away, 0.0)
        grad = jnp.dot(miss, classes, precision=lax.Precision.HIGHEST, preferred_element_type=F32)
        grad = grad[:1] / (GRID * GRID)
        st[0] = jnp.where(last > 0, jnp.broadcast_to(grad, last.shape), 0.0).astype(BF)
        st[1] = jnp.zeros((ROWS, CH), BF)

    def twin_of(cell):
        a, b, s = parts_of(cell)
        return remote(gw.at[1 - core, a, b, s], rb.at[a, b, s], send, recv, cell, near["core"])

    def join(cell):
        a, b, s = parts_of(cell)
        twin_of(cell).wait_recv()
        gw[core, a, b, s] = (gw[core, a, b, s].astype(F32) + rb[a, b, s].astype(F32)).astype(BF)

    def cell_backward(i, g, wgrad):
        cell = CELLS - 1 - i
        a_, b_, s_ = parts_of(cell)
        total = tt[cell]
        q = lax.rsqrt(jnp.mean(total * total, axis=-1, keepdims=True) + EPSILON)
        n = total * q
        gn = g[0].astype(F32)
        on = holds(cell)
        gt = q * (gn - n * jnp.mean(gn * n, axis=-1, keepdims=True))
        gt = jnp.where(on, gt, 0.0)
        gh = gt.astype(BF)
        gs[...] = lax.dot_general(gh, w_ref[1, cell], NT, preferred_element_type=F32)
        gm = lax.dot_general(gh, w_ref[0, cell], NT, preferred_element_type=F32)
        prev = sp[cell]
        g[0] = jnp.where(on, gt + jnp.where(prev > 0, gm, 0.0) + g[1].astype(F32), gn).astype(BF)
        for c in range(4):
            cols = slice(128 * c, 128 * c + 128)
            u_ = gs[:, cols]
            k = s_ref[cell, :, cols].astype(F32)
            gv = [pltpu.roll(u_, ROWS - 1, 0), u_, pltpu.roll(u_, 1, 0)]
            r = [
                k[3 * u : 3 * u + 1] * gv[0] + k[3 * u + 1 : 3 * u + 2] * gv[1] + k[3 * u + 2 : 3 * u + 3] * gv[2]
                for u in range(3)
            ]
            rel = r[1] + up(r[0]) + down(r[2])
            older = so[cell, :, cols].astype(F32)
            g[1, :, cols] = jnp.where(holds(cell, cols), jnp.where(older > 0, rel, 0.0), g[1, :, cols].astype(F32)).astype(BF)
            if wgrad:
                a = jnp.maximum(older, 0.0)
                for v in range(3):
                    taps[v : v + 1, cols] = jnp.sum(a[:-PITCH] * gv[v][PITCH:], axis=0, keepdims=True)
                    taps[3 + v : 4 + v, cols] = jnp.sum(a * gv[v], axis=0, keepdims=True)
                    taps[6 + v : 7 + v, cols] = jnp.sum(a[PITCH:] * gv[v][:-PITCH], axis=0, keepdims=True)
        if wgrad:
            tk[a_, b_, s_] = taps[...].astype(BF)
            parts = (8, 2, 2, 16, CH)
            gw[0, a_, b_, s_] = (
                lax.dot_general(jnp.maximum(prev, 0), gh, TN, preferred_element_type=F32).astype(BF).reshape(parts)
            )
            gw[1, a_, b_, s_] = lax.dot_general(ss[cell], gh, TN, preferred_element_type=F32).astype(BF).reshape(parts)
            twin_of(cell).start()

            @pl.when(i >= 1)
            def _():
                join(cell + 1)

            for at, steps in during.items():

                @pl.when(i == at)
                def _(steps=steps):
                    for way, *at_step in steps:
                        way(*at_step)

        return 0

    acc = gw.at[core]
    table = {}

    def define(key, make):
        table[key] = (make, count[0])
        count[0] += 1

    def copy(key):
        make, index = table[key]
        source, target, name = make()
        return remote(source, target, send, recv, index, near[name])

    def start(*keys):
        for key in keys:
            copy(key).start()

    def wait(*keys):
        for key in keys:
            copy(key).wait_recv()

    def zat(d):
        return (z + 8 + d) % 8

    def xat(d):
        x = (xh * 2 + xl + 4 + d) % 4
        return x // 2, x % 2

    def a1(g, b, s, d):
        return acc.at[g, b, s, zat(d), 0]

    def b1(g, s, d):
        h, l = xat(d)
        return acc.at[g, h, s, :, 1, l]

    def a2(g, d):
        h, l = xat(d)
        return acc.at[g, h, :, z, 0, l]

    def b2(g, d):
        return acc.at[g, xh, :, zat(d), 1, xl]

    def plus(ref, *others):
        v = ref[...].astype(F32)
        for o in others:
            v = v + o[...].astype(F32)
        ref[...] = v.astype(BF)

    def straight(g, b):
        return g == 0 and b == 0

    SIGN = (1, -1)
    ZDIR, XDIR = ("z+", "z-"), ("x+", "x-")
    PART = (pl.ds(0, 2), pl.ds(2, 1))
    for g in (1, 0):
        for w in range(2):
            half = pl.ds(4 * w, 4)
            for s in range(3):
                for b in range(2):
                    if not straight(g, b):
                        define(
                            ("za", g, b, s, 0, w),
                            lambda g=g, b=b, s=s, w=w: (a1(g, b, s, 4).at[w], zp0.at[g, w, b, s], ZDIR[w]),
                        )
                    elif w == 0:
                        define(("z4", g, b, s), lambda g=g, b=b, s=s: (a1(g, b, s, 4), zp0.at[g, :, b, s], "z4"))
                    for k in (1, 2, 3):
                        define(
                            ("za", g, b, s, k, w),
                            lambda g=g, b=b, s=s, w=w, k=k: (
                                a1(g, b, s, SIGN[w] * (4 - k)),
                                zp.at[g, k - 1, w, b, s],
                                ZDIR[w],
                            ),
                        )
                define(
                    ("xb", g, s, 0, w), lambda g=g, s=s, w=w, half=half: (b1(g, s, 2).at[half], xp0.at[g, w, s], XDIR[w])
                )
                define(("xb", g, s, 1, w), lambda g=g, s=s, w=w: (b1(g, s, SIGN[w]), xp.at[g, w, s], XDIR[w]))
            define(("xa", g, 1, w), lambda g=g, w=w: (a2(g, SIGN[w]), ap.at[g, w], XDIR[w]))
            for k in (1, 2, 3):
                define(("zb", g, k, w), lambda g=g, w=w, k=k: (b2(g, SIGN[w] * (4 - k)), bp.at[g, k - 1, w], ZDIR[w]))
        define(("xa2", g), lambda g=g: (a2(g, 2), ap0.at[g], "x2"))
        define(("zb4", g), lambda g=g: (b2(g, 4), bp0.at[g], "z4"))
    for c in range(2):
        define(("y", c), lambda c=c: (acc.at[1 - yl, xh, :, z, c, xl], yb.at[c], "y"))

    def both(*key):
        return (*key, 0), (*key, 1)

    def ring_z(g, b, s, k):
        if k == 1 and straight(g, b):
            start(*both("za", g, b, s, 1))
            start(("z4", g, b, s))
        elif k == 1:
            start(*both("za", g, b, s, 0))
        elif k > 2 or not straight(g, b):
            wait(*both("za", g, b, s, k - 2))
            for w in range(2):
                if k == 2:
                    plus(a1(g, b, s, SIGN[w] * 3).at[w], zp0.at[g, w, b, s])
                else:
                    plus(a1(g, b, s, SIGN[w] * (5 - k)), zp.at[g, k - 3, w, b, s])
            start(*both("za", g, b, s, k - 1))

    def ring_x(g, s, k):
        if k == 1:
            start(*both("xb", g, s, 0))
        else:
            wait(*both("xb", g, s, 0))
            for w in range(2):
                plus(b1(g, s, SIGN[w]).at[pl.ds(4 * w, 4)], xp0.at[g, w, s])
            start(*both("xb", g, s, 1))

    def along_z(g, k):
        if k == 5:
            for s in range(3):
                for b in range(2):
                    wait(*both("za", g, b, s, 3))
                    if straight(g, b):
                        wait(("z4", g, b, s))
                        plus(a1(g, b, s, 0), zp.at[g, 2, 0, b, s], zp.at[g, 2, 1, b, s], zp0.at[g, :, b, s])
                    else:
                        plus(a1(g, b, s, 0), zp.at[g, 2, 0, b, s], zp.at[g, 2, 1, b, s])
            start(*both("xa", g, 1))
            start(("xa2", g))
        else:
            wait(*both("xa", g, 1))
            wait(("xa2", g))
            plus(a2(g, 0), ap.at[g, 0], ap.at[g, 1], ap0.at[g])

            @pl.when(yl != g)
            def _():
                start(("y", 0))

    def along_x(g, k):
        if k == 3:
            for s in range(3):
                wait(*both("xb", g, s, 1))
                plus(b1(g, s, 0), xp.at[g, 0, s], xp.at[g, 1, s])
            start(*both("zb", g, 1))
            start(("zb4", g))
        elif k <= 6:
            wait(*both("zb", g, k - 4))
            for w in range(2):
                plus(b2(g, SIGN[w] * (7 - k)), bp.at[g, k - 5, w])
            start(*both("zb", g, k - 3))
        else:
            wait(*both("zb", g, 3))
            wait(("zb4", g))
            plus(b2(g, 0), bp.at[g, 2, 0], bp.at[g, 2, 1], bp0.at[g])

            @pl.when(yl != g)
            def _():
                start(("y", 1))

    def z_(n, k):
        cell = CELLS - 1 - n
        ring_z(cell // 6, (cell // 3) % 2, cell % 3, k)

    x_ = ring_x
    during = {at: [] for at in range(1, CELLS)}
    left = {}
    for n in range(CELLS):
        left[n] = []
        for k, late in enumerate(Z_LATE, 1):
            if n >= 9 and k == 2:
                continue
            if n + late < CELLS:
                during[n + late].append((z_, n, k))
            else:
                left[n].append(k)
    for at, args in enumerate(((1, 2, 1), (1, 1, 1), (1, 0, 1))):
        during[4 + at].append((x_, *args))
    for at, args in enumerate(((1, 2, 2), (1, 1, 2), (1, 0, 2))):
        during[X_LATE + at].append((x_, *args))
    during[10].append((x_, 0, 2, 1))
    during[11].append((x_, 0, 1, 1))

    def z_round():
        for n in range(CELLS):
            if left[n]:
                z_(n, left[n].pop(0))

    taps[...] = jnp.zeros_like(taps)

    @pl.when(stage == 1)
    def _():
        for c in hops:
            c.wait_recv()
        for i in range(2):
            spread(hi[i].astype(F32), st, i)

    lax.fori_loop(0, CELLS, cell_forward, 0)

    @pl.when(stage == 0)
    def _():
        for i in range(2):
            ho[i] = packed(st, i)
            hops[i].start()
        for i in range(2):
            hops[i].wait_recv()
            spread(hi[i].astype(F32), gb, i)

    @pl.when(stage == 1)
    def _():
        head()
        gb[...] = st[...]
        lax.fori_loop(0, CELLS, lambda i, _: cell_backward(i, st, False), 0)
        for i in range(2):
            ho[i] = packed(st, i)
            hops[i].start()

    lax.fori_loop(0, CELLS, lambda i, _: cell_backward(i, gb, True), 0)
    join(jnp.int32(0))
    z_(11, left[11].pop(0))
    x_(0, 0, 1)
    step = move(tk, tr, "core")

    def fold(dst, a, b):
        for s in range(3):
            dst[s] = (a[s].astype(F32) + b[s].astype(F32)).astype(BF)

    z_round()
    x_(0, 2, 2)
    x_(0, 1, 2)
    along_x(1, 3)
    step.wait_recv()
    for a in range(2):
        for b in range(2):
            fold(tr.at[a, b], tr.at[a, b], tk.at[a, b])
    step = move(tr.at[1 - yl], ty, "y")
    x_(0, 0, 2)
    z_round()
    step.wait_recv()
    for b in range(2):
        fold(ty.at[b], ty.at[b], tr.at[yl, b])
    step = move(ty.at[1 - xh], tx.at[0], "xd")
    along_x(1, 5)
    z_round()
    along_z(1, 5)
    step.wait_recv()
    fold(tx.at[0], tx.at[0], ty.at[xh])
    step = move(tx.at[0], tx.at[1], "xs")
    along_x(0, 3)
    along_x(1, 6)
    while any(left.values()):
        z_round()
    along_z(1, 7)
    step.wait_recv()
    fold(tz.at[0, 0], tx.at[0], tx.at[1])
    step = [move(tz.at[0, 0], tz.at[1, 0], "z+"), move(tz.at[0, 0], tz.at[1, 1], "z-")]
    along_x(0, 5)
    along_z(0, 5)
    along_x(1, 7)
    along_x(0, 6)
    for c in step:
        c.wait_recv()
    step = [move(tz.at[1, 0], tz.at[2, 0], "z+"), move(tz.at[1, 1], tz.at[2, 1], "z-")]
    along_z(0, 7)

    def landed(c):
        wait(("y", c))
        for s in range(3):
            ob[core, s, z, c, xl] = (acc[yl, xh, s, z, c, xl].astype(F32) + yb[c, s].astype(F32)).astype(BF)

    last = []

    def to(at, name):
        return move(at, at, name)

    def to_twin(at):
        last.append(to(at, "core"))

    def piece(c, d):
        return ob.at[core, :, zat(d), c, xl]

    def arrived(copies):
        for c in copies:
            c.wait_recv()

    out = [None, None]
    side = []

    def beside(c, d):
        side.append((c, d, to(piece(c, d), "xs")))

    def first(c):
        landed(c)
        out[c] = [to(piece(c, 0), "z+"), to(piece(c, 0), "z-")]
        beside(c, 0)

    def next_one(c, k):
        arrived(out[c])
        if k < 3:
            out[c] = [to(piece(c, -k), "z+"), to(piece(c, k), "z-")]
        else:
            out[c] = [to(piece(c, -3).at[PART[0]], "z+"), to(piece(c, 3).at[PART[1]], "z-")]
        beside(c, -k)
        beside(c, k)

    def settle(n):
        for c, d, copy_of in side[:n]:
            copy_of.wait_recv()
            last.append(to(ob.at[core, :, zat(d), c], "core"))
        del side[:n]

    first(0)
    along_x(0, 7)
    first(1)
    arrived(step)
    step = [move(tz.at[2, 0], tz.at[3, 0], "z+"), move(tz.at[2, 1], tz.at[3, 1], "z-")]
    next_one(0, 1)
    next_one(1, 1)
    settle(2)
    next_one(0, 2)
    next_one(1, 2)
    settle(4)
    arrived(step)
    step = move(tz.at[3, 0], tz.at[4, 0], "z+")
    next_one(0, 3)
    next_one(1, 3)
    settle(4)
    for c in range(2):
        arrived(out[c])
        beside(c, 4)
    settle(6)
    step.wait_recv()
    for s in range(3):
        v = tz[0, 0, s].astype(F32) + tz[4, 0, s].astype(F32)
        for k in (1, 2, 3):
            v = v + tz[k, 0, s].astype(F32) + tz[k, 1, s].astype(F32)
        t_ref[s] = v
    done = [pltpu.make_async_copy(ob.at[core], o_ref.at[core], local.at[0])]
    done[0].start()
    arrived(last)
    done.append(pltpu.make_async_copy(ob.at[1 - core], o_ref.at[1 - core], local.at[1]))
    done[1].start()
    for c in done:
        c.wait()
    assert count[0] <= SEMAPHORES
    for c in sends:
        c.wait_send()
    for c in hops:
        c.wait_send()
    for key in table:
        copy(key).wait_send()

    def sent(cell, _):
        twin_of(cell).wait_send()
        return 0

    lax.fori_loop(0, CELLS, sent, 0)


def shards(features, labels, classifier, w_mix, w_point, kernels, counts):
    lead = (16, CH)
    shape = lambda *d: pltpu.VMEM(d + lead, BF)
    maps = lambda n, t=BF: pltpu.VMEM((n, ROWS, CH), t)
    n = SEMAPHORES
    summed, taps = pl.pallas_call(
        kernel,
        out_shape=(jax.ShapeDtypeStruct((2, 3, 8, 2, 2, 16, CH), BF), jax.ShapeDtypeStruct((3, 16, CH), F32)),
        in_specs=[pl.BlockSpec(memory_space=pl.ANY)] * 4
        + [pl.BlockSpec(memory_space=pltpu.VMEM)]
        + [pl.BlockSpec(memory_space=pltpu.SMEM)] * 2,
        out_specs=(pl.BlockSpec(memory_space=pl.ANY), pl.BlockSpec(memory_space=pltpu.VMEM)),
        scratch_shapes=[
            pltpu.VMEM((2, CELLS, CH, CH), BF),
            pltpu.VMEM((CELLS, 16, CH), BF),
            pltpu.VMEM((GRID * GRID, CH), BF),
            pltpu.VMEM((3, 9, CH), BF),
            maps(2),
            maps(2),
            pltpu.VMEM((2, GRID * GRID, CH), BF),
            pltpu.VMEM((2, GRID * GRID, CH), BF),
            maps(CELLS),
            maps(CELLS),
            maps(CELLS),
            maps(CELLS, F32),
            pltpu.VMEM((ROWS, CH), F32),
            pltpu.VMEM((16, CH), F32),
            shape(2, 2, 2, 3, 8, 2, 2),
            shape(2, 2, 3, 8, 2, 2),
            shape(2, 2, 3),
            shape(2, 2, 3),
            shape(2, 3),
            shape(2, 3),
            shape(5, 2, 3),
            shape(2, 2, 2, 3),
            shape(2, 3, 2, 2, 3, 2),
            shape(2, 2, 3, 4),
            shape(2, 2, 3, 8),
            shape(2, 3),
            shape(2, 2, 3),
            shape(2, 3),
            shape(2, 3, 2, 3),
            shape(2, 3),
            shape(2, 3, 8, 2, 2),
            pltpu.SemaphoreType.DMA((n,)),
            pltpu.SemaphoreType.DMA((n,)),
            pltpu.SemaphoreType.DMA((4,)),
        ],
        compiler_params=pltpu.CompilerParams(collective_id=1, has_side_effects=True, vmem_limit_bytes=VMEM_MB << 20),
        name="step",
    )(features, w_mix, w_point, kernels, classifier.T, labels, counts)
    summed = summed.reshape(2, 3, CH, CH).astype(F32)
    return summed[0], summed[1], taps[:, :9]


def solution(mesh):
    return jax.shard_map(
        shards,
        mesh=mesh,
        in_specs=(
            P("dp", None, None),
            P("dp"),
            P(),
            P("segment", None, None),
            P("segment", None, None),
            P("segment", None, None),
            P("segment"),
        ),
        out_specs=(P("segment", None, None), P("segment", None, None), P("segment", None, None)),
        check_vma=False,
    )
```

```python
import jax
import jax.numpy as jnp
from jax import lax
from jax.experimental import pallas as pl
from jax.experimental.pallas import tpu as pltpu
from jax.sharding import PartitionSpec as P

GRID = 12
PITCH = 16
ROWS = GRID * PITCH
CH = 512
CELLS = 12
EPSILON = 1e-06
MESH = pl.DeviceIdType.MESH
VMEM_MB = 62
SEMAPHORES = 300
Z_LATE = (1, 3, 5, 7)
X_LATE = 7
BF = jnp.bfloat16
F32 = jnp.float32


def place():
    seg, dp = lax.axis_index("segment"), lax.axis_index("dp")
    y, xh = seg // 2, seg % 2
    core, xl, z = dp % 2, (dp // 2) % 2, dp // 4
    return seg, dp, y, xh, z, xl, core


def dev(y, xh, z, xl, core):
    return (y * 2 + xh, (z * 2 + xl) * 2 + core)


def neighbours():
    seg, dp, y, xh, z, xl, core = place()
    yp = y + 1 - 2 * (y % 2)
    return {
        "core": dev(y, xh, z, xl, 1 - core),
        "xs": dev(y, xh, z, 1 - xl, core),
        "xd": dev(y, 1 - xh, z, 1 - xl, core),
        "x+": dev(y, jnp.where(xl == 0, xh, 1 - xh), z, 1 - xl, core),
        "x-": dev(y, jnp.where(xl == 1, xh, 1 - xh), z, 1 - xl, core),
        "z+": dev(y, xh, (z + 1) % 8, xl, core),
        "z-": dev(y, xh, (z + 7) % 8, xl, core),
        "z4": dev(y, xh, (z + 4) % 8, xl, core),
        "x2": dev(y, 1 - xh, z, xl, core),
        "y": dev(yp, xh, z, xl, core),
        "hop": dev(3 - y, xh, z, xl, core),
    }


def greet(names, near):
    barrier = pltpu.get_barrier_semaphore()
    for name in names:
        pl.semaphore_signal(barrier, inc=1, device_id=near[name], device_id_type=MESH)
    pl.semaphore_wait(barrier, len(names))


def remote(src, dst, send, recv, i, target):
    return pltpu.make_async_remote_copy(
        src_ref=src, dst_ref=dst, send_sem=send.at[i], recv_sem=recv.at[i], device_id=target, device_id_type=MESH
    )


def down(r):
    return jnp.concatenate([jnp.zeros((PITCH, r.shape[1]), r.dtype), r[:-PITCH]], axis=0)


def up(r):
    return jnp.concatenate([r[PITCH:], jnp.zeros((PITCH, r.shape[1]), r.dtype)], axis=0)


NT = (((1,), (1,)), ((), ()))
TN = (((0,), (0,)), ((), ()))


def parts_of(cell):
    return cell // 6, (cell // 3) % 2, cell % 3


def kernel(
    f_ref, mix_ref, point_ref, tap_ref, class_ref, label_ref, count_ref, o_ref, t_ref,
    w_ref, s_ref, img, tin, st, gb, ho, hi, sp, so, ss, tt, gs, taps, gw, rb,
    tk, tr, ty, tx, tz, zp0, zp, xp0, xp, ap0, ap, bp0, bp, yb, ob, send, recv, local,
):
    _, _, y, xh, z, xl, core = place()
    near = neighbours()
    stage, yl, zpar = y // 2, y % 2, z % 2
    image = jnp.where(stage == 0, y, 3 - y) * 2 + xh
    own = yl * 2 + xh
    sec_y, sec_x, sec_xy = (1 - yl) * 2 + xh, yl * 2 + (1 - xh), (1 - yl) * 2 + (1 - xh)
    count = [14]
    sends = []

    def move(src, dst, name):
        c = remote(src, dst, send, recv, count[0], near[name])
        count[0] += 1
        sends.append(c)
        c.start()
        return c

    def spread(pixels, dst, i):
        for r in range(GRID):
            row = jnp.concatenate([pixels[GRID * r : GRID * r + GRID], jnp.zeros((PITCH - GRID, CH), F32)], axis=0)
            dst[i, PITCH * r : PITCH * r + PITCH] = row.astype(BF)

    def packed(maps, i):
        pixels = maps[i].astype(F32)
        return jnp.concatenate([pixels[PITCH * r : PITCH * r + GRID] for r in range(GRID)], axis=0).astype(BF)

    loc = [
        pltpu.make_async_copy(tap_ref, tin, local.at[2]),
        pltpu.make_async_copy(mix_ref, w_ref.at[0, pl.ds(own * 3, 3)], local.at[0]),
        pltpu.make_async_copy(point_ref, w_ref.at[1, pl.ds(own * 3, 3)], local.at[1]),
        pltpu.make_async_copy(f_ref.at[image], img, local.at[3]),
    ]
    for c in loc:
        c.start()
    greet(("core", "xs", "xd", "z+", "z-", "z4", "x2", "y", "hop"), near)
    for c in loc:
        c.wait()
    many = jnp.full((7, CH), count_ref[0].astype(F32), F32)
    for s in range(3):
        s_ref[own * 3 + s] = jnp.concatenate([tin[s].astype(F32), many], axis=0).astype(BF)

    def go(sec, slot, row, count, name):
        at = w_ref.at[core, sec * 3 + slot, pl.ds(pl.multiple_of(row, 16), count)]
        return move(at, at, name)

    def tiny(sec, name):
        at = s_ref.at[pl.ds(sec * 3, 3)]
        return move(at, at, name)

    mine, other = 128 * (2 * zpar + xl), 128 * (2 * zpar + 1 - xl)

    def to_z(sec, slot, row):
        return [go(sec, slot, row, 64, "z+"), go(sec, slot, row + 64, 64, "z-")]

    t_y, t_x = tiny(own, "y"), tiny(own, "xd")
    x1, y_first, y_then, x2, xy1, xy2, zx, zy, zxy, twin = [], [], [], [], [], [], [], [], [], []
    for s in range(3):
        x1.append(go(own, s, other, 128, "xd"))
        y_first.append(go(own, s, other, 128, "y"))
    for s in range(3):
        y_then.append(go(own, s, mine, 128, "y"))
    y_rest = go(own, 2, 256 * (1 - zpar), 256, "y")
    t_y.wait_recv()
    t_xy = tiny(sec_y, "xd")
    for s in range(3):
        x1[s].wait_recv()
        x2.append(go(sec_x, s, mine, 128, "xs"))
        zx.append(to_z(sec_x, s, mine))
        y_first[s].wait_recv()
        xy1.append(go(sec_y, s, other, 128, "xd"))
        zy.append(to_z(sec_y, s, other) if s < 2 else [y_rest])
    for s in range(3):
        x2[s].wait_recv()
        zx[s] += to_z(sec_x, s, other)
        twin.append(go(sec_x, s, 256 * zpar, 256, "core"))
    for s in range(3):
        xy1[s].wait_recv()
        xy2.append(go(sec_xy, s, mine, 128, "xs"))
        zxy.append(to_z(sec_xy, s, mine))
        y_then[s].wait_recv()
        if s < 2:
            zy[s] += to_z(sec_y, s, mine)
        twin.append(go(sec_y, s, 256 * zpar, 256, "core"))
    for s in range(3):
        xy2[s].wait_recv()
        zxy[s] += to_z(sec_xy, s, other)
        twin.append(go(sec_xy, s, 256 * zpar, 256, "core"))
    for sec, group in ((sec_x, zx), (sec_y, zy), (sec_xy, zxy)):
        for s in range(3):
            for c in group[s]:
                c.wait_recv()
            twin.append(go(sec, s, 256 * (1 - zpar), 256, "core"))

    image_in = img[...].astype(F32)
    spread(image_in, st, 0)
    spread(image_in, st, 1)
    for c in twin + [t_x, t_xy]:
        c.wait_recv()

    hops = [remote(ho.at[i], hi.at[i], send, recv, 12 + i, near["hop"]) for i in range(2)]
    real = lax.broadcasted_iota(jnp.int32, (ROWS, 128), 0) % PITCH < GRID

    def holds(cell, cols=slice(None)):
        return s_ref[cell, 9:10, cols].astype(F32) > (cell % 3).astype(F32)

    def cell_forward(cell, _):
        sp[cell] = st[0]
        so[cell] = st[1]
        for c in range(4):
            cols = slice(128 * c, 128 * c + 128)
            a = jnp.maximum(st[1, :, cols].astype(F32), 0.0)
            k = s_ref[cell, :, cols].astype(F32)
            am, ap_ = pltpu.roll(a, 1, 0), pltpu.roll(a, ROWS - 1, 0)
            r = [k[3 * u : 3 * u + 1] * am + k[3 * u + 1 : 3 * u + 2] * a + k[3 * u + 2 : 3 * u + 3] * ap_ for u in range(3)]
            s = r[1] + down(r[0]) + up(r[2])
            ss[cell, :, cols] = jnp.where(real, s, 0.0).astype(BF)
        prev = st[0]
        total = jnp.dot(ss[cell], w_ref[1, cell], preferred_element_type=F32)
        total = total + jnp.dot(jnp.maximum(prev, 0), w_ref[0, cell], preferred_element_type=F32)
        prev = prev.astype(F32)
        total = prev + total
        q = lax.rsqrt(jnp.mean(total * total, axis=-1, keepdims=True) + EPSILON)
        tt[cell] = total
        on = holds(cell)
        st[1] = jnp.where(on, prev, st[1].astype(F32)).astype(BF)
        st[0] = jnp.where(on, total * q, prev).astype(BF)
        return 0

    def head():
        last = st[0].astype(F32)
        pooled = jnp.sum(jnp.maximum(last, 0.0), axis=0, keepdims=True) / (GRID * GRID)
        pooled = jnp.broadcast_to(pooled, (8, CH))
        classes = class_ref[...]
        logits = lax.dot_general(pooled, classes, NT, precision=lax.Precision.HIGHEST, preferred_element_type=F32)
        label = label_ref[image].astype(F32)
        away = jnp.abs(lax.broadcasted_iota(jnp.int32, logits.shape, 1).astype(F32) - label)
        miss = logits - jnp.maximum(1.0 - away, 0.0)
        grad = jnp.dot(miss, classes, precision=lax.Precision.HIGHEST, preferred_element_type=F32)
        grad = grad[:1] / (GRID * GRID)
        st[0] = jnp.where(last > 0, jnp.broadcast_to(grad, last.shape), 0.0).astype(BF)
        st[1] = jnp.zeros((ROWS, CH), BF)

    def twin_of(cell):
        a, b, s = parts_of(cell)
        return remote(gw.at[1 - core, a, b, s], rb.at[a, b, s], send, recv, cell, near["core"])

    def join(cell):
        a, b, s = parts_of(cell)
        twin_of(cell).wait_recv()
        gw[core, a, b, s] = (gw[core, a, b, s].astype(F32) + rb[a, b, s].astype(F32)).astype(BF)

    def cell_backward(i, g, wgrad):
        cell = CELLS - 1 - i
        a_, b_, s_ = parts_of(cell)
        total = tt[cell]
        q = lax.rsqrt(jnp.mean(total * total, axis=-1, keepdims=True) + EPSILON)
        n = total * q
        gn = g[0].astype(F32)
        on = holds(cell)
        gt = q * (gn - n * jnp.mean(gn * n, axis=-1, keepdims=True))
        gt = jnp.where(on, gt, 0.0)
        gh = gt.astype(BF)
        gs[...] = lax.dot_general(gh, w_ref[1, cell], NT, preferred_element_type=F32)
        gm = lax.dot_general(gh, w_ref[0, cell], NT, preferred_element_type=F32)
        prev = sp[cell]
        g[0] = jnp.where(on, gt + jnp.where(prev > 0, gm, 0.0) + g[1].astype(F32), gn).astype(BF)
        for c in range(4):
            cols = slice(128 * c, 128 * c + 128)
            u_ = gs[:, cols]
            k = s_ref[cell, :, cols].astype(F32)
            gv = [pltpu.roll(u_, ROWS - 1, 0), u_, pltpu.roll(u_, 1, 0)]
            r = [
                k[3 * u : 3 * u + 1] * gv[0] + k[3 * u + 1 : 3 * u + 2] * gv[1] + k[3 * u + 2 : 3 * u + 3] * gv[2]
                for u in range(3)
            ]
            rel = r[1] + up(r[0]) + down(r[2])
            older = so[cell, :, cols].astype(F32)
            g[1, :, cols] = jnp.where(holds(cell, cols), jnp.where(older > 0, rel, 0.0), g[1, :, cols].astype(F32)).astype(BF)
            if wgrad:
                a = jnp.maximum(older, 0.0)
                for v in range(3):
                    taps[v : v + 1, cols] = jnp.sum(a[:-PITCH] * gv[v][PITCH:], axis=0, keepdims=True)
                    taps[3 + v : 4 + v, cols] = jnp.sum(a * gv[v], axis=0, keepdims=True)
                    taps[6 + v : 7 + v, cols] = jnp.sum(a[PITCH:] * gv[v][:-PITCH], axis=0, keepdims=True)
        if wgrad:
            tk[a_, b_, s_] = taps[...].astype(BF)
            parts = (8, 2, 2, 16, CH)
            gw[0, a_, b_, s_] = (
                lax.dot_general(jnp.maximum(prev, 0), gh, TN, preferred_element_type=F32).astype(BF).reshape(parts)
            )
            gw[1, a_, b_, s_] = lax.dot_general(ss[cell], gh, TN, preferred_element_type=F32).astype(BF).reshape(parts)
            twin_of(cell).start()

            @pl.when(i >= 1)
            def _():
                join(cell + 1)

            for at, steps in during.items():

                @pl.when(i == at)
                def _(steps=steps):
                    for way, *at_step in steps:
                        way(*at_step)

        return 0

    acc = gw.at[core]
    table = {}

    def define(key, make):
        table[key] = (make, count[0])
        count[0] += 1

    def copy(key):
        make, index = table[key]
        source, target, name = make()
        return remote(source, target, send, recv, index, near[name])

    def start(*keys):
        for key in keys:
            copy(key).start()

    def wait(*keys):
        for key in keys:
            copy(key).wait_recv()

    def zat(d):
        return (z + 8 + d) % 8

    def xat(d):
        x = (xh * 2 + xl + 4 + d) % 4
        return x // 2, x % 2

    def a1(g, b, s, d):
        return acc.at[g, b, s, zat(d), 0]

    def b1(g, s, d):
        h, l = xat(d)
        return acc.at[g, h, s, :, 1, l]

    def a2(g, d):
        h, l = xat(d)
        return acc.at[g, h, :, z, 0, l]

    def b2(g, d):
        return acc.at[g, xh, :, zat(d), 1, xl]

    def plus(ref, *others):
        v = ref[...].astype(F32)
        for o in others:
            v = v + o[...].astype(F32)
        ref[...] = v.astype(BF)

    def straight(g, b):
        return g == 0 and b == 0

    SIGN = (1, -1)
    ZDIR, XDIR = ("z+", "z-"), ("x+", "x-")
    PART = (pl.ds(0, 2), pl.ds(2, 1))
    for g in (1, 0):
        for w in range(2):
            half = pl.ds(4 * w, 4)
            for s in range(3):
                for b in range(2):
                    if not straight(g, b):
                        define(
                            ("za", g, b, s, 0, w),
                            lambda g=g, b=b, s=s, w=w: (a1(g, b, s, 4).at[w], zp0.at[g, w, b, s], ZDIR[w]),
                        )
                    elif w == 0:
                        define(("z4", g, b, s), lambda g=g, b=b, s=s: (a1(g, b, s, 4), zp0.at[g, :, b, s], "z4"))
                    for k in (1, 2, 3):
                        define(
                            ("za", g, b, s, k, w),
                            lambda g=g, b=b, s=s, w=w, k=k: (
                                a1(g, b, s, SIGN[w] * (4 - k)),
                                zp.at[g, k - 1, w, b, s],
                                ZDIR[w],
                            ),
                        )
                define(
                    ("xb", g, s, 0, w), lambda g=g, s=s, w=w, half=half: (b1(g, s, 2).at[half], xp0.at[g, w, s], XDIR[w])
                )
                define(("xb", g, s, 1, w), lambda g=g, s=s, w=w: (b1(g, s, SIGN[w]), xp.at[g, w, s], XDIR[w]))
            define(("xa", g, 1, w), lambda g=g, w=w: (a2(g, SIGN[w]), ap.at[g, w], XDIR[w]))
            for k in (1, 2, 3):
                define(("zb", g, k, w), lambda g=g, w=w, k=k: (b2(g, SIGN[w] * (4 - k)), bp.at[g, k - 1, w], ZDIR[w]))
        define(("xa2", g), lambda g=g: (a2(g, 2), ap0.at[g], "x2"))
        define(("zb4", g), lambda g=g: (b2(g, 4), bp0.at[g], "z4"))
    for c in range(2):
        define(("y", c), lambda c=c: (acc.at[1 - yl, xh, :, z, c, xl], yb.at[c], "y"))

    def both(*key):
        return (*key, 0), (*key, 1)

    def ring_z(g, b, s, k):
        if k == 1 and straight(g, b):
            start(*both("za", g, b, s, 1))
            start(("z4", g, b, s))
        elif k == 1:
            start(*both("za", g, b, s, 0))
        elif k > 2 or not straight(g, b):
            wait(*both("za", g, b, s, k - 2))
            for w in range(2):
                if k == 2:
                    plus(a1(g, b, s, SIGN[w] * 3).at[w], zp0.at[g, w, b, s])
                else:
                    plus(a1(g, b, s, SIGN[w] * (5 - k)), zp.at[g, k - 3, w, b, s])
            start(*both("za", g, b, s, k - 1))

    def ring_x(g, s, k):
        if k == 1:
            start(*both("xb", g, s, 0))
        else:
            wait(*both("xb", g, s, 0))
            for w in range(2):
                plus(b1(g, s, SIGN[w]).at[pl.ds(4 * w, 4)], xp0.at[g, w, s])
            start(*both("xb", g, s, 1))

    def along_z(g, k):
        if k == 5:
            for s in range(3):
                for b in range(2):
                    wait(*both("za", g, b, s, 3))
                    if straight(g, b):
                        wait(("z4", g, b, s))
                        plus(a1(g, b, s, 0), zp.at[g, 2, 0, b, s], zp.at[g, 2, 1, b, s], zp0.at[g, :, b, s])
                    else:
                        plus(a1(g, b, s, 0), zp.at[g, 2, 0, b, s], zp.at[g, 2, 1, b, s])
            start(*both("xa", g, 1))
            start(("xa2", g))
        else:
            wait(*both("xa", g, 1))
            wait(("xa2", g))
            plus(a2(g, 0), ap.at[g, 0], ap.at[g, 1], ap0.at[g])

            @pl.when(yl != g)
            def _():
                start(("y", 0))

    def along_x(g, k):
        if k == 3:
            for s in range(3):
                wait(*both("xb", g, s, 1))
                plus(b1(g, s, 0), xp.at[g, 0, s], xp.at[g, 1, s])
            start(*both("zb", g, 1))
            start(("zb4", g))
        elif k <= 6:
            wait(*both("zb", g, k - 4))
            for w in range(2):
                plus(b2(g, SIGN[w] * (7 - k)), bp.at[g, k - 5, w])
            start(*both("zb", g, k - 3))
        else:
            wait(*both("zb", g, 3))
            wait(("zb4", g))
            plus(b2(g, 0), bp.at[g, 2, 0], bp.at[g, 2, 1], bp0.at[g])

            @pl.when(yl != g)
            def _():
                start(("y", 1))

    def z_(n, k):
        cell = CELLS - 1 - n
        ring_z(cell // 6, (cell // 3) % 2, cell % 3, k)

    x_ = ring_x
    during = {at: [] for at in range(1, CELLS)}
    left = {}
    for n in range(CELLS):
        left[n] = []
        for k, late in enumerate(Z_LATE, 1):
            if n >= 9 and k == 2:
                continue
            if n + late < CELLS:
                during[n + late].append((z_, n, k))
            else:
                left[n].append(k)
    for at, args in enumerate(((1, 2, 1), (1, 1, 1), (1, 0, 1))):
        during[4 + at].append((x_, *args))
    for at, args in enumerate(((1, 2, 2), (1, 1, 2), (1, 0, 2))):
        during[X_LATE + at].append((x_, *args))
    during[10].append((x_, 0, 2, 1))
    during[11].append((x_, 0, 1, 1))

    def z_round():
        for n in range(CELLS):
            if left[n]:
                z_(n, left[n].pop(0))

    taps[...] = jnp.zeros_like(taps)

    @pl.when(stage == 1)
    def _():
        for c in hops:
            c.wait_recv()
        for i in range(2):
            spread(hi[i].astype(F32), st, i)

    lax.fori_loop(0, CELLS, cell_forward, 0)

    @pl.when(stage == 0)
    def _():
        for i in range(2):
            ho[i] = packed(st, i)
            hops[i].start()
        for i in range(2):
            hops[i].wait_recv()
            spread(hi[i].astype(F32), gb, i)

    @pl.when(stage == 1)
    def _():
        head()
        gb[...] = st[...]
        lax.fori_loop(0, CELLS, lambda i, _: cell_backward(i, st, False), 0)
        for i in range(2):
            ho[i] = packed(st, i)
            hops[i].start()

    lax.fori_loop(0, CELLS, lambda i, _: cell_backward(i, gb, True), 0)
    join(jnp.int32(0))
    z_(11, left[11].pop(0))
    x_(0, 0, 1)
    step = move(tk, tr, "core")

    def fold(dst, a, b):
        for s in range(3):
            dst[s] = (a[s].astype(F32) + b[s].astype(F32)).astype(BF)

    z_round()
    x_(0, 2, 2)
    x_(0, 1, 2)
    along_x(1, 3)
    step.wait_recv()
    for a in range(2):
        for b in range(2):
            fold(tr.at[a, b], tr.at[a, b], tk.at[a, b])
    step = move(tr.at[1 - yl], ty, "y")
    x_(0, 0, 2)
    z_round()
    step.wait_recv()
    for b in range(2):
        fold(ty.at[b], ty.at[b], tr.at[yl, b])
    step = move(ty.at[1 - xh], tx.at[0], "xd")
    along_x(1, 5)
    z_round()
    along_z(1, 5)
    step.wait_recv()
    fold(tx.at[0], tx.at[0], ty.at[xh])
    step = move(tx.at[0], tx.at[1], "xs")
    along_x(0, 3)
    along_x(1, 6)
    while any(left.values()):
        z_round()
    along_z(1, 7)
    step.wait_recv()
    fold(tz.at[0, 0], tx.at[0], tx.at[1])
    step = [move(tz.at[0, 0], tz.at[1, 0], "z+"), move(tz.at[0, 0], tz.at[1, 1], "z-")]
    along_x(0, 5)
    along_z(0, 5)
    along_x(1, 7)
    along_x(0, 6)
    for c in step:
        c.wait_recv()
    step = [move(tz.at[1, 0], tz.at[2, 0], "z+"), move(tz.at[1, 1], tz.at[2, 1], "z-")]
    along_z(0, 7)

    def landed(c):
        wait(("y", c))
        for s in range(3):
            ob[core, s, z, c, xl] = (acc[yl, xh, s, z, c, xl].astype(F32) + yb[c, s].astype(F32)).astype(BF)

    last = []

    def to(at, name):
        return move(at, at, name)

    def to_twin(at):
        last.append(to(at, "core"))

    def piece(c, d):
        return ob.at[core, :, zat(d), c, xl]

    def arrived(copies):
        for c in copies:
            c.wait_recv()

    out = [None, None]
    side = []

    def beside(c, d):
        side.append((c, d, to(piece(c, d), "xs")))

    def first(c):
        landed(c)
        out[c] = [to(piece(c, 0), "z+"), to(piece(c, 0), "z-")]
        beside(c, 0)

    def next_one(c, k):
        arrived(out[c])
        if k < 3:
            out[c] = [to(piece(c, -k), "z+"), to(piece(c, k), "z-")]
        else:
            out[c] = [to(piece(c, -3).at[PART[0]], "z+"), to(piece(c, 3).at[PART[1]], "z-")]
        beside(c, -k)
        beside(c, k)

    def settle(n):
        for c, d, copy_of in side[:n]:
            copy_of.wait_recv()
            last.append(to(ob.at[core, :, zat(d), c], "core"))
        del side[:n]

    first(0)
    along_x(0, 7)
    first(1)
    arrived(step)
    step = [move(tz.at[2, 0], tz.at[3, 0], "z+"), move(tz.at[2, 1], tz.at[3, 1], "z-")]
    next_one(0, 1)
    next_one(1, 1)
    settle(2)
    next_one(0, 2)
    next_one(1, 2)
    settle(4)
    arrived(step)
    step = move(tz.at[3, 0], tz.at[4, 0], "z+")
    next_one(0, 3)
    next_one(1, 3)
    settle(4)
    for c in range(2):
        arrived(out[c])
        beside(c, 4)
    settle(6)
    step.wait_recv()
    for s in range(3):
        v = tz[0, 0, s].astype(F32) + tz[4, 0, s].astype(F32)
        for k in (1, 2, 3):
            v = v + tz[k, 0, s].astype(F32) + tz[k, 1, s].astype(F32)
        t_ref[s] = v
    done = [pltpu.make_async_copy(ob.at[core], o_ref.at[core], local.at[0])]
    done[0].start()
    arrived(last)
    done.append(pltpu.make_async_copy(ob.at[1 - core], o_ref.at[1 - core], local.at[1]))
    done[1].start()
    for c in done:
        c.wait()
    assert count[0] <= SEMAPHORES
    for c in sends:
        c.wait_send()
    for c in hops:
        c.wait_send()
    for key in table:
        copy(key).wait_send()

    def sent(cell, _):
        twin_of(cell).wait_send()
        return 0

    lax.fori_loop(0, CELLS, sent, 0)


def widen_kernel(x_ref, t_ref, mix_ref, point_ref, tap_ref):
    mix_ref[...] = x_ref[0].astype(F32)
    point_ref[...] = x_ref[1].astype(F32)

    @pl.when(pl.program_id(0) == 0)
    def _():
        for s in range(3):
            for tap in range(9):
                tap_ref[tap, s : s + 1] = t_ref[s, tap : tap + 1]


def widen(summed, taps):
    out = pl.BlockSpec((1, CH, CH), lambda i: (i, 0, 0))
    whole = jax.ShapeDtypeStruct((3, CH, CH), F32)
    return pl.pallas_call(
        widen_kernel,
        grid=(3,),
        in_specs=[
            pl.BlockSpec((2, 1, CH, CH), lambda i: (0, i, 0, 0)),
            pl.BlockSpec((3, 16, CH), lambda i: (0, 0, 0)),
        ],
        out_specs=[out, out, pl.BlockSpec((9, 3, CH), lambda i: (0, 0, 0))],
        out_shape=[whole, whole, jax.ShapeDtypeStruct((9, 3, CH), F32)],
        name="widen",
    )(summed, taps)


def shards(features, labels, classifier, w_mix, w_point, kernels, counts):
    lead = (16, CH)
    shape = lambda *d: pltpu.VMEM(d + lead, BF)
    maps = lambda n, t=BF: pltpu.VMEM((n, ROWS, CH), t)
    n = SEMAPHORES
    summed, taps = pl.pallas_call(
        kernel,
        out_shape=(jax.ShapeDtypeStruct((2, 3, 8, 2, 2, 16, CH), BF), jax.ShapeDtypeStruct((3, 16, CH), F32)),
        in_specs=[pl.BlockSpec(memory_space=pl.ANY)] * 4
        + [pl.BlockSpec(memory_space=pltpu.VMEM)]
        + [pl.BlockSpec(memory_space=pltpu.SMEM)] * 2,
        out_specs=(pl.BlockSpec(memory_space=pl.ANY), pl.BlockSpec(memory_space=pltpu.VMEM)),
        scratch_shapes=[
            pltpu.VMEM((2, CELLS, CH, CH), BF),
            pltpu.VMEM((CELLS, 16, CH), BF),
            pltpu.VMEM((GRID * GRID, CH), BF),
            pltpu.VMEM((3, 9, CH), BF),
            maps(2),
            maps(2),
            pltpu.VMEM((2, GRID * GRID, CH), BF),
            pltpu.VMEM((2, GRID * GRID, CH), BF),
            maps(CELLS),
            maps(CELLS),
            maps(CELLS),
            maps(CELLS, F32),
            pltpu.VMEM((ROWS, CH), F32),
            pltpu.VMEM((16, CH), F32),
            shape(2, 2, 2, 3, 8, 2, 2),
            shape(2, 2, 3, 8, 2, 2),
            shape(2, 2, 3),
            shape(2, 2, 3),
            shape(2, 3),
            shape(2, 3),
            shape(5, 2, 3),
            shape(2, 2, 2, 3),
            shape(2, 3, 2, 2, 3, 2),
            shape(2, 2, 3, 4),
            shape(2, 2, 3, 8),
            shape(2, 3),
            shape(2, 2, 3),
            shape(2, 3),
            shape(2, 3, 2, 3),
            shape(2, 3),
            shape(2, 3, 8, 2, 2),
            pltpu.SemaphoreType.DMA((n,)),
            pltpu.SemaphoreType.DMA((n,)),
            pltpu.SemaphoreType.DMA((4,)),
        ],
        compiler_params=pltpu.CompilerParams(collective_id=1, has_side_effects=True, vmem_limit_bytes=VMEM_MB << 20),
        name="step",
    )(features, w_mix, w_point, kernels, classifier.T, labels, counts)
    mix, point, taps = widen(summed.reshape(2, 3, CH, CH), taps)
    return mix, point, taps.transpose(1, 0, 2)


def solution(mesh):
    return jax.shard_map(
        shards,
        mesh=mesh,
        in_specs=(
            P("dp", None, None),
            P("dp"),
            P(),
            P("segment", None, None),
            P("segment", None, None),
            P("segment", None, None),
            P("segment"),
        ),
        out_specs=(P("segment", None, None), P("segment", None, None), P("segment", None, None)),
        check_vma=False,
    )
```
